256 devices in a mesh: ctx: 64 (over z_lo, x, y, core), dp: 4 (over z_hi).
Axes of the slice: x: 4, y: 4, z: 8 (z_hi: 4, z_lo: 2; z = z_hi * 2 + z_lo), core: 2. Of those that a mesh axis runs over, the one named last changes fastest.
Arguments:
- hidden: bfloat16 [4, 8192, 1024], P('dp', 'ctx'), may hold values from -6 to 6
- depth: int32 [4, 8192], P('dp', 'ctx'), may hold values from 1 to 3, as said below
- cotangent: bfloat16 [4, 8192, 1024], P('dp', 'ctx'), may hold values from -6 to 6
- embeds: float32 [2, 1024], replicated, may hold values from -4 to 4
- mods: float32 [2, 3, 1024], replicated, may hold values from -4 to 4
- w_query: bfloat16 [1024, 1024], replicated, may hold values from -0.1875 to 0.1875
- w_key: bfloat16 [1024, 1024], replicated, may hold values from -0.1875 to 0.1875
- w_value: bfloat16 [1024, 1024], replicated, may hold values from -0.1875 to 0.1875
- w_out: bfloat16 [1024, 1024], replicated, may hold values from -0.1875 to 0.1875
Outputs:
- grad_hidden: bfloat16 [4, 8192, 1024], P('dp', 'ctx')
- grad_query: float32 [1024, 1024], P('ctx')
- grad_key: float32 [1024, 1024], P('ctx')
- grad_value: float32 [1024, 1024], P('ctx')
- grad_out: float32 [1024, 1024], P('ctx')
- grad_embeds: float32 [2, 1024], replicated
- grad_mods: float32 [2, 3, 1024], replicated
The draws below stay inside these ranges and needn't reach their ends.
Inputs may be any that keep to these rules, and one draw needn't show every extreme that they name: Within the tokens of one device (each aligned block of 128 positions) between 6 and 12 tokens have depth 2 or more, exactly 12 in at least one block of every draw; each block holds at least one token of depth 3.
All inputs are finite; a program needn't handle non-finite values.
Results may differ from the reference program's by a relative error of at most 0.028.
Values may be sent and summed in bfloat16 or wider, within the bound.
No kernel may reach another device: no remote copies, remote signals or barrier semaphores. Data moves between devices by JAX's collectives and lax.ppermute only.
A program may use at most 128 MiB of HBM per device.

```python
import jax
import jax.numpy as jnp
from jax import lax

D = 1024
H = 8
DH = 128
HD = 1024
TOK_DEV = 128
CAP = 12
LEN = 8192
SEQS = 4
N_CTX = 64


def draw_depth(key, part):
    key = jax.random.fold_in(key, 11)
    blocks = SEQS * (LEN // TOK_DEV)
    count_key, fullest_key, deeper_key, order_key = jax.random.split(key, 4)
    reaching = jax.random.randint(count_key, (blocks,), CAP // 2, CAP + 1)
    fullest = jax.random.randint(fullest_key, (), 0, blocks)
    reaching = jnp.where(jnp.arange(blocks) == fullest, CAP, reaching)
    deeper = jnp.minimum(jax.random.randint(deeper_key, (blocks,), max(1, CAP // 4), CAP // 2 + 1), reaching)
    scores = jax.random.randint(order_key, (blocks, TOK_DEV), 0, 1 << 20) * TOK_DEV + jnp.arange(TOK_DEV, dtype=jnp.int32)[None, :]
    ranking = jnp.argsort(jnp.argsort(scores, axis=1), axis=1)
    levels = 1 + (ranking < reaching[:, None]).astype(jnp.int32) + (ranking < deeper[:, None]).astype(jnp.int32)
    return levels.reshape(SEQS, LEN).astype(jnp.int32)


def steps_of(rng, dims, pieces, low, top_value):
    level, own = 1.0, jax.random.fold_in(rng, 6)
    for position, blocks in pieces:
        heights = jnp.exp(jax.random.uniform(jax.random.fold_in(own, position), (blocks,), jnp.float32, low / len(pieces), top_value / len(pieces)))
        level = level * jnp.repeat(heights, dims[position] // blocks).reshape([-1 if axis == position else 1 for axis in range(len(dims))])
    return level


def gaussian(stream_key, extent, scale, limit, cuts=(), held_as=jnp.bfloat16):
    loudness = steps_of(stream_key, extent, cuts, -0.22, 0.18) if cuts else 1.0
    values = jax.random.normal(stream_key, extent, jnp.float32) * scale * loudness
    return jnp.minimum(jnp.maximum(values, -limit), limit).astype(held_as)


def setup_inputs(seed: int = 0) -> dict:
    seeds = jax.random.split(jax.random.key(seed), 10)
    return {
        "hidden": gaussian(seeds[0], (SEQS, LEN, D), 1.0, 6.0, ((0, 4), (1, 64))),
        "depth": draw_depth(jax.random.fold_in(seeds[9], 71), 0),
        "cotangent": gaussian(seeds[2], (SEQS, LEN, D), 1.0, 6.0, ((0, 4), (1, 64))),
        "embeds": gaussian(seeds[3], (2, D), 0.5, 4.0, (), jnp.float32),
        "mods": gaussian(seeds[4], (2, 3, D), 0.5, 4.0, (), jnp.float32),
        "w_query": gaussian(seeds[5], (D, HD), D ** -0.5, 0.1875),
        "w_key": gaussian(seeds[6], (D, HD), D ** -0.5, 0.1875),
        "w_value": gaussian(seeds[7], (D, HD), D ** -0.5, 0.1875),
        "w_out": gaussian(seeds[8], (HD, D), HD ** -0.5, 0.1875),
    }


EPSILON = 1e-06
NEGATIVE = -1e+30
EXACT = lax.Precision.HIGHEST

def slot_table(active, slot_count):
    placing = jnp.cumsum(active.astype(jnp.int32), axis=-1) - 1
    slot_ids = jnp.arange(slot_count, dtype=jnp.int32)
    return (active[..., None] & (placing[..., None] == slot_ids)).astype(jnp.float32)

def take_rows(picker, stream):
    gathered = jnp.einsum('btc,btd->bcd', picker, stream.astype(jnp.float32), precision=EXACT)
    return gathered.reshape(-1, stream.shape[-1])

def put_rows(picker, slot_rows):
    blocks, length, slot_count = picker.shape
    return jnp.einsum('btc,bcd->btd', picker, slot_rows.reshape(blocks, slot_count, -1), precision=EXACT)

def sequence_pass(stream, depths, upstream, embeds, mods, w_query, w_key, w_value, w_out):
    stream = stream.reshape(N_CTX, TOK_DEV, D)
    depths = depths.reshape(N_CTX, TOK_DEV)
    upstream = upstream.reshape(N_CTX, TOK_DEV, D).astype(jnp.float32)
    score_scale = DH ** (-0.5)
    records = []
    for section in range(2):
        picker = slot_table(depths >= section + 2, CAP)
        filled = lax.optimization_barrier(jnp.sum(picker, axis=1)).reshape(-1)
        key_count = filled.shape[0]
        slot_index = jnp.arange(key_count, dtype=jnp.int32)
        allowed = (filled > 0)[None, :] & (slot_index[None, :] <= slot_index[:, None]) | (slot_index[None, :] == slot_index[:, None])
        slot_rows = take_rows(picker, stream)
        shifted = slot_rows + embeds[section]
        factor = lax.rsqrt(lax.optimization_barrier(jnp.mean(shifted * shifted, axis=-1, keepdims=True)) + EPSILON)
        normed = shifted * factor
        mod_row = mods[section]
        inputs = (normed * (1.0 + mod_row[1]) + mod_row[0]).astype(jnp.bfloat16)
        queries = jnp.dot(inputs, w_query, preferred_element_type=jnp.float32).astype(jnp.bfloat16)
        key_rows = jnp.dot(inputs, w_key, preferred_element_type=jnp.float32).astype(jnp.bfloat16)
        value_rows = jnp.dot(inputs, w_value, preferred_element_type=jnp.float32).astype(jnp.bfloat16)
        query_heads = queries.reshape(key_count, H, DH).astype(jnp.float32)
        key_heads = key_rows.reshape(key_count, H, DH).astype(jnp.float32)
        value_heads = value_rows.reshape(key_count, H, DH).astype(jnp.float32)
        scores = jnp.einsum('qhd,khd->hqk', query_heads, key_heads) * score_scale
        masked = jnp.where(allowed[None], scores, NEGATIVE)
        highest = lax.optimization_barrier(jnp.max(masked, axis=-1))
        log_total = highest + jnp.log(lax.optimization_barrier(jnp.sum(jnp.exp(masked - highest[..., None]), axis=-1)))
        softmax = jnp.exp(masked - log_total[..., None])
        softmax_low = softmax.astype(jnp.bfloat16)
        outputs = jnp.einsum('hqk,khd->qhd', softmax_low.astype(jnp.float32), value_heads).reshape(key_count, HD).astype(jnp.bfloat16)
        branch = jnp.dot(outputs, w_out, preferred_element_type=jnp.float32)
        stream = (stream.astype(jnp.float32) + put_rows(picker, mod_row[2] * branch)).astype(jnp.bfloat16)
        records.append((picker, normed, factor, inputs, query_heads, key_heads, value_heads, softmax, softmax_low, outputs, branch))
    sums = [jnp.zeros((D, HD), jnp.float32) for item in range(3)] + [jnp.zeros((HD, D), jnp.float32)]
    embed_grads = []
    mod_grads = []
    for section in (1, 0):
        picker, normed, factor, inputs, query_heads, key_heads, value_heads, softmax, softmax_low, outputs, branch = records[section]
        mod_row = mods[section]
        key_count = inputs.shape[0]
        slot_grads = take_rows(picker, upstream)
        gate_grad = lax.optimization_barrier(jnp.sum(slot_grads * branch, axis=0))
        mixed_grad = (slot_grads * mod_row[2]).astype(jnp.bfloat16)
        out_grad = jnp.dot(mixed_grad, w_out.T, preferred_element_type=jnp.float32).astype(jnp.bfloat16)
        grad_heads = out_grad.reshape(key_count, H, DH).astype(jnp.float32)
        output_heads = outputs.reshape(key_count, H, DH).astype(jnp.float32)
        row_inner = jnp.einsum('qhd,qhd->hq', grad_heads, output_heads)
        prob_grads = jnp.einsum('qhd,khd->hqk', grad_heads, value_heads)
        score_grads = (softmax * (prob_grads - row_inner[..., None]) * DH ** (-0.5)).astype(jnp.bfloat16).astype(jnp.float32)
        query_grad = jnp.einsum('hqk,khd->qhd', score_grads, key_heads).reshape(key_count, HD).astype(jnp.bfloat16)
        key_grad = jnp.einsum('hqk,qhd->khd', score_grads, query_heads).reshape(key_count, HD).astype(jnp.bfloat16)
        value_grad = jnp.einsum('hqk,qhd->khd', softmax_low.astype(jnp.float32), grad_heads).reshape(key_count, HD).astype(jnp.bfloat16)
        input_grads = jnp.dot(query_grad, w_query.T, preferred_element_type=jnp.float32)
        input_grads = input_grads + jnp.dot(key_grad, w_key.T, preferred_element_type=jnp.float32)
        input_grads = input_grads + jnp.dot(value_grad, w_value.T, preferred_element_type=jnp.float32)
        sums[0] = sums[0] + jnp.dot(inputs.T, query_grad, preferred_element_type=jnp.float32)
        sums[1] = sums[1] + jnp.dot(inputs.T, key_grad, preferred_element_type=jnp.float32)
        sums[2] = sums[2] + jnp.dot(inputs.T, value_grad, preferred_element_type=jnp.float32)
        sums[3] = sums[3] + jnp.dot(outputs.T, mixed_grad, preferred_element_type=jnp.float32)
        shift_grad = lax.optimization_barrier(jnp.sum(input_grads, axis=0))
        scale_grad = lax.optimization_barrier(jnp.sum(input_grads * normed, axis=0))
        normed_grad = input_grads * (1.0 + mod_row[1])
        shifted_grad = factor * (normed_grad - normed * lax.optimization_barrier(jnp.mean(normed_grad * normed, axis=-1, keepdims=True)))
        embed_grads.insert(0, lax.optimization_barrier(jnp.sum(shifted_grad, axis=0)))
        mod_grads.insert(0, jnp.stack([shift_grad, scale_grad, gate_grad]))
        upstream = upstream + put_rows(picker, shifted_grad)
    return (upstream.reshape(LEN, D), sums, jnp.stack(embed_grads), jnp.stack(mod_grads))

def reference(hidden, depth, cotangent, embeds, mods, w_query, w_key, w_value, w_out):
    grad_rows = []
    totals = None
    for sequence in range(hidden.shape[0]):
        upstream, sums, embed_grads, mod_grads = sequence_pass(hidden[sequence], depth[sequence], cotangent[sequence], embeds, mods, w_query, w_key, w_value, w_out)
        grad_rows.append(upstream.astype(jnp.bfloat16))
        current = sums + [embed_grads, mod_grads]
        totals = current if totals is None else [former + latter for former, latter in zip(totals, current)]
    grad_hidden = jnp.stack(grad_rows)
    return (grad_hidden, totals[0], totals[1], totals[2], totals[3], totals[4], totals[5])
```

```python
import functools

import jax
import jax.numpy as jnp
from jax import lax
from jax.experimental import pallas as pl
from jax.experimental.pallas import tpu as pltpu
from jax.sharding import Mesh, PartitionSpec as P

D = 1024
H = 8
DH = 128
TOK = 128
CAP = 12
N_CTX = 64
CHIPS = 32
SLOTS = 768
HALF = 512
HEADS = 4
WIDE = D + 128
BLK = 256
NBLK = SLOTS // BLK
EPSILON = 1e-06
NEGATIVE = -1e30
EMPTY = 64.0
SCALE = DH ** (-0.5)
SCALE2 = SCALE * 1.4426950408889634
VMEM_LIMIT = 56 * 1024 * 1024
BF = jnp.bfloat16
F32 = jnp.float32

VSPEC = pl.BlockSpec(memory_space=pltpu.VMEM)
SSPEC = pl.BlockSpec(memory_space=pltpu.SMEM)
HSPEC = pl.BlockSpec(memory_space=pl.ANY)


def nn(a, b):
    return lax.dot_general(a, b, (((1,), (0,)), ((), ())), preferred_element_type=F32)


def nt(a, b):
    return lax.dot_general(a, b, (((1,), (1,)), ((), ())), preferred_element_type=F32)


def tn(a, b):
    return lax.dot_general(a, b, (((0,), (0,)), ((), ())), preferred_element_type=F32)


def sds(shape, dtype):
    return jax.ShapeDtypeStruct(shape, dtype)


def call(kernel, out_shape, in_specs, scratch=(), out_specs=None):
    if out_specs is None:
        out_specs = jax.tree.map(lambda _: VSPEC, out_shape)
    return pl.pallas_call(
        kernel,
        out_shape=out_shape,
        in_specs=in_specs,
        out_specs=out_specs,
        scratch_shapes=list(scratch),
        compiler_params=pltpu.CompilerParams(vmem_limit_bytes=VMEM_LIMIT),
    )


def pick_kernel(depth_ref, hidden_ref, cot_ref, payload_ref, picker_ref):
    depth = jnp.broadcast_to(depth_ref[...], (16, TOK))
    active = depth >= 2
    before = lax.broadcasted_iota(jnp.int32, (TOK, TOK), 0)
    upto = lax.broadcasted_iota(jnp.int32, (TOK, TOK), 1)
    upper = jnp.where(before <= upto, 1.0, 0.0).astype(BF)
    placing = nn(jnp.where(active, 1.0, 0.0).astype(BF), upper) - 1.0
    slot = lax.broadcasted_iota(jnp.int32, (16, TOK), 0)
    hit = active & (placing == slot.astype(F32)) & (slot < CAP)
    picker = jnp.where(hit, 1.0, 0.0)
    picker_ref[...] = picker.astype(BF)
    level = jnp.sum(picker * (depth - 1).astype(F32), axis=1, keepdims=True)
    rows = nn(picker.astype(BF), hidden_ref[0])
    rows = jnp.where(level > 0.5, rows, EMPTY)
    grads = nn(picker.astype(BF), cot_ref[0])
    level_wide = jnp.broadcast_to(level, (16, 128))
    payload_ref[0:CAP, 0:D] = rows[0:CAP]
    payload_ref[0:CAP, D:WIDE] = level_wide[0:CAP]
    payload_ref[CAP : 2 * CAP, 0:D] = grads[0:CAP]
    payload_ref[CAP : 2 * CAP, D:WIDE] = level_wide[0:CAP]


def pick(depth, hidden, cotangent):
    return call(
        pick_kernel,
        (sds((2 * CAP, WIDE), F32), sds((16, TOK), BF)),
        [VSPEC, VSPEC, VSPEC],
    )(depth, hidden, cotangent)


def causal_bias():
    key = lax.broadcasted_iota(jnp.int32, (BLK, BLK), 0)
    query = lax.broadcasted_iota(jnp.int32, (BLK, BLK), 1)
    return jnp.where(key <= query, 0.0, NEGATIVE).astype(F32)


def norm_rows(u):
    factor = lax.rsqrt(jnp.mean(u * u, axis=-1, keepdims=True) + EPSILON)
    return factor, u * factor


def biased_scores(k, q, bias_ref, causal, upto):
    s = nt(k, q)
    bias = bias_ref[0:upto, :]
    s = s + jnp.concatenate([bias, bias], axis=1)
    last = s[upto - BLK : upto] + causal
    if upto == BLK:
        return last
    return jnp.concatenate([s[: upto - BLK], last], axis=0)


def attention_forward(q_ref, k_ref, v_ref, o_ref, lse_ref, bias_ref):
    causal = causal_bias()
    for head in range(HEADS):
        cols = slice(head * DH, (head + 1) * DH)
        vt = v_ref[:, cols].T
        for block in range(NBLK):
            upto = (block + 1) * BLK
            rows = slice(block * BLK, upto)
            s = biased_scores(k_ref[0:upto, cols], q_ref[rows, cols], bias_ref, causal, upto)
            top = jnp.max(s, axis=0, keepdims=True)
            e = jnp.exp2((s - top) * SCALE2)
            total = jnp.sum(e, axis=0, keepdims=True)
            ot = nn(vt[:, 0:upto], e.astype(BF)) * (1.0 / total)
            o_ref[rows, cols] = ot.T.astype(BF)
            lse_ref[head : head + 1, rows] = jnp.maximum(top * SCALE2 + jnp.log2(total), -1e25)


def attention_backward(
    q_ref, k_ref, v_ref, o_ref, do_ref, lse_ref, bias_ref, dq_ref, dk_ref, dv_ref, dk_acc, dv_acc
):
    causal = causal_bias()
    for head in range(HEADS):
        cols = slice(head * DH, (head + 1) * DH)
        kt = k_ref[:, cols].T
        for block in range(NBLK - 1, -1, -1):
            upto = (block + 1) * BLK
            rows = slice(block * BLK, upto)
            q = q_ref[rows, cols]
            do = do_ref[rows, cols]
            inner = jnp.sum((do.astype(F32) * o_ref[rows, cols].astype(F32)).T, axis=0, keepdims=True)
            s = biased_scores(k_ref[0:upto, cols], q, bias_ref, causal, upto)
            p = jnp.exp2(s * SCALE2 - lse_ref[head : head + 1, rows])
            dp = nt(v_ref[0:upto, cols], do)
            ds = (p * (dp - inner)).astype(BF)
            dv_part = nn(p.astype(BF), do)
            dk_part = nn(ds, q)
            if block == NBLK - 1:
                dv_acc[...] = dv_part
                dk_acc[...] = dk_part
            else:
                dv_acc[0:upto] += dv_part
                dk_acc[0:upto] += dk_part
            dqt = nn(kt[:, 0:upto], ds)
            dq_ref[rows, cols] = (dqt.T * SCALE).astype(BF)
        dk_ref[:, cols] = (dk_acc[...] * SCALE).astype(BF)
        dv_ref[:, cols] = dv_acc[...].astype(BF)


def project(x, rows, wq, wk, wv, q_ref, k_ref, v_ref):
    q_ref[rows, :] = nn(x, wq[...]).astype(BF)
    k_ref[rows, :] = nn(x, wk[...]).astype(BF)
    v_ref[rows, :] = nn(x, wv[...]).astype(BF)


def unproject(rows, wq, wk, wv, dq_ref, dk_ref, dv_ref):
    return nt(dq_ref[rows, :], wq[...]) + nt(dk_ref[rows, :], wk[...]) + nt(dv_ref[rows, :], wv[...])


def half_copies(core, weights, scratches, sems):
    start = pl.multiple_of(core * HALF, HALF)
    return [
        pltpu.make_async_copy(w.at[:, pl.ds(start, HALF)], s, sems.at[i])
        for i, (w, s) in enumerate(zip(weights, scratches))
    ]


def weight_grads(core, chip, x_ref, o_ref, dy_ref, dq_ref, dk_ref, dv_ref, grads):
    strip = pl.multiple_of((chip // 4) * DH, DH)
    xs = x_ref[:, pl.ds(strip, DH)]
    grads[:, 0:HALF] = tn(xs, dq_ref[...])
    grads[:, HALF : 2 * HALF] = tn(xs, dk_ref[...])
    grads[:, 2 * HALF : 3 * HALF] = tn(xs, dv_ref[...])
    own = jnp.where(chip // 16 == core, 1.0, 0.0).astype(F32)
    o_strip = pl.multiple_of(((chip // 4) % 4) * DH, DH)
    os = o_ref[:, pl.ds(o_strip, DH)]
    grads[:, 3 * HALF :] = tn(os, dy_ref[...]) * own


def first_kernel(
    ids_ref, own_ref, other_ref, embeds_ref, mods_ref, wq_hbm, wk_hbm, wv_hbm,
    q_ref, k_ref, v_ref, o_ref, lse_ref, h_ref, g_ref, level_ref,
    wq, wk, wv, even, odd, hs, gs, bias, sems,
):
    core = ids_ref[0]
    copies = half_copies(core, (wq_hbm, wk_hbm, wv_hbm), (wq, wk, wv), sems)
    for copy in copies:
        copy.start()
    is_even = core == 0

    def place(chip, carry):
        mine = own_ref[chip].astype(F32)
        theirs = other_ref[chip].astype(F32)
        even[...] = jnp.where(is_even, mine, theirs)
        odd[...] = jnp.where(is_even, theirs, mine)
        base = pl.multiple_of(chip * 2 * CAP, 8)
        block_h = hs.at[pl.ds(base, 2 * CAP)]
        block_g = gs.at[pl.ds(base, 2 * CAP)]
        block_h[0:CAP] = even[0:CAP]
        block_h[CAP : 2 * CAP] = odd[0:CAP]
        block_g[0:CAP] = even[CAP : 2 * CAP]
        block_g[CAP : 2 * CAP] = odd[CAP : 2 * CAP]
        return carry

    lax.fori_loop(0, CHIPS, place, 0)
    level = hs[:, D:WIDE]
    level_ref[...] = level
    bias[...] = jnp.where(level > 0.5, 0.0, NEGATIVE)
    g_ref[...] = gs[:, 0:D].astype(BF)
    h_ref[...] = hs[:, 0:D].astype(BF)
    for copy in copies:
        copy.wait()
    embed = embeds_ref[0:1, :]
    shift = mods_ref[0:1, :]
    scale = 1.0 + mods_ref[1:2, :]
    for block in range(NBLK):
        rows = slice(block * BLK, (block + 1) * BLK)
        factor, normed = norm_rows(hs[rows, 0:D] + embed)
        x = (normed * scale + shift).astype(BF)
        project(x, rows, wq, wk, wv, q_ref, k_ref, v_ref)
    attention_forward(q_ref, k_ref, v_ref, o_ref, lse_ref, bias)


def first(ids, own, other, embeds, mods, wq, wk, wv):
    half = sds((SLOTS, HALF), BF)
    full = sds((SLOTS, D), BF)
    return call(
        first_kernel,
        (half, half, half, half, sds((8, SLOTS), F32), full, full, sds((SLOTS, 128), F32)),
        [SSPEC, VSPEC, VSPEC, VSPEC, VSPEC, HSPEC, HSPEC, HSPEC],
        [
            pltpu.VMEM((D, HALF), BF),
            pltpu.VMEM((D, HALF), BF),
            pltpu.VMEM((D, HALF), BF),
            pltpu.VMEM((2 * CAP, WIDE), F32),
            pltpu.VMEM((2 * CAP, WIDE), F32),
            pltpu.VMEM((SLOTS, WIDE), F32),
            pltpu.VMEM((SLOTS, WIDE), F32),
            pltpu.VMEM((SLOTS, 128), F32),
            pltpu.SemaphoreType.DMA((3,)),
        ],
    )(ids, own, other, embeds, mods, wq, wk, wv)


def second_kernel(
    ids_ref, o_own_ref, o_other_ref, h_ref, g_ref, level_ref, embeds_ref, mods_ref,
    wq_hbm, wk_hbm, wv_hbm, wo_hbm,
    dx_ref, h1_ref, y0_ref, grads_ref, gate_ref,
    wq, wk, wv, wo, x_ref, q_ref, k_ref, v_ref, o_ref, lse_ref, dy_ref, do_ref,
    dq_ref, dk_ref, dv_ref, dk_acc, dv_acc, grads, bias, sems,
):
    core = ids_ref[0]
    chip = ids_ref[1]
    wo_copy = pltpu.make_async_copy(wo_hbm, wo, sems.at[3])
    wo_copy.start()
    copies = half_copies(core, (wq_hbm, wk_hbm, wv_hbm), (wq, wk, wv), sems)
    for copy in copies:
        copy.start()
    bias[...] = jnp.where(level_ref[...] > 1.5, 0.0, NEGATIVE)
    wo_copy.wait()
    for copy in copies:
        copy.wait()
    own_rows = pl.ds(pl.multiple_of(core * HALF, HALF), HALF)
    other_rows = pl.ds(pl.multiple_of((1 - core) * HALF, HALF), HALF)
    gate0 = mods_ref[2:3, :]
    embed = embeds_ref[1:2, :]
    shift = mods_ref[3:4, :]
    scale = 1.0 + mods_ref[4:5, :]
    gate1 = mods_ref[5:6, :]
    for block in range(NBLK):
        rows = slice(block * BLK, (block + 1) * BLK)
        y0 = nn(o_own_ref[rows, :], wo[own_rows, :]) + nn(o_other_ref[rows, :], wo[other_rows, :])
        y0_ref[rows, :] = y0.astype(BF)
        h1 = (h_ref[rows, :].astype(F32) + gate0 * y0).astype(BF)
        h1_ref[rows, :] = h1
        factor, normed = norm_rows(h1.astype(F32) + embed)
        x = (normed * scale + shift).astype(BF)
        x_ref[rows, :] = x
        project(x, rows, wq, wk, wv, q_ref, k_ref, v_ref)
        deep = jnp.where(level_ref[rows, 0:1] > 1.5, 1.0, 0.0)
        dy = (g_ref[rows, :].astype(F32) * deep * gate1).astype(BF)
        dy_ref[rows, :] = dy
        do_ref[rows, :] = nt(dy, wo[own_rows, :]).astype(BF)
    attention_forward(q_ref, k_ref, v_ref, o_ref, lse_ref, bias)
    attention_backward(
        q_ref, k_ref, v_ref, o_ref, do_ref, lse_ref, bias, dq_ref, dk_ref, dv_ref, dk_acc, dv_acc
    )
    gate_sum = jnp.zeros((1, D), F32)
    for block in range(NBLK):
        rows = slice(block * BLK, (block + 1) * BLK)
        dx_ref[rows, :] = unproject(rows, wq, wk, wv, dq_ref, dk_ref, dv_ref).astype(BF)
        y1 = nn(o_ref[rows, :], wo[own_rows, :])
        deep = jnp.where(level_ref[rows, 0:1] > 1.5, 1.0, 0.0)
        gate_sum += jnp.sum(g_ref[rows, :].astype(F32) * deep * y1, axis=0, keepdims=True)
    gate_ref[...] = jnp.broadcast_to(gate_sum, (8, D))
    weight_grads(core, chip, x_ref, o_ref, dy_ref, dq_ref, dk_ref, dv_ref, grads)
    grads_ref[...] = grads[pl.ds(pl.multiple_of((chip % 4) * 32, 32), 32), :]


def second(ids, o_own, o_other, h, g, level, embeds, mods, wq, wk, wv, wo):
    full = sds((SLOTS, D), BF)
    half = pltpu.VMEM((SLOTS, HALF), BF)
    weight = pltpu.VMEM((D, HALF), BF)
    return call(
        second_kernel,
        (full, full, full, sds((32, 5 * HALF), F32), sds((8, D), F32)),
        [SSPEC] + [VSPEC] * 7 + [HSPEC] * 4,
        [
            weight, weight, weight, pltpu.VMEM((D, D), BF),
            pltpu.VMEM((SLOTS, D), BF), half, half, half, half,
            pltpu.VMEM((8, SLOTS), F32), pltpu.VMEM((SLOTS, D), BF), half,
            half, half, half,
            pltpu.VMEM((SLOTS, DH), F32), pltpu.VMEM((SLOTS, DH), F32),
            pltpu.VMEM((DH, 5 * HALF), F32), pltpu.VMEM((SLOTS, 128), F32),
            pltpu.SemaphoreType.DMA((4,)),
        ],
    )(ids, o_own, o_other, h, g, level, embeds, mods, wq, wk, wv, wo)


def third_kernel(
    ids_ref, dx_own_ref, dx_other_ref, h1_ref, h_ref, g_ref, level_ref, y0_ref,
    q_ref, k_ref, v_ref, o_ref, lse_ref, grads1_ref, gate1_ref, embeds_ref, mods_ref,
    wq_hbm, wk_hbm, wv_hbm, wo_hbm,
    keep_ref, send_ref, mine_ref,
    wq, wk, wv, wo, x_ref, dy_ref, do_ref, dq_ref, dk_ref, dv_ref, dk_acc, dv_acc, grads,
    bias, gs, dx0, sums, sems,
):
    core = ids_ref[0]
    chip = ids_ref[1]
    own_rows = pl.ds(pl.multiple_of(core * HALF, HALF), HALF)
    wo_copy = pltpu.make_async_copy(wo_hbm.at[own_rows, :], wo, sems.at[3])
    wo_copy.start()
    copies = half_copies(core, (wq_hbm, wk_hbm, wv_hbm), (wq, wk, wv), sems)
    for copy in copies:
        copy.start()
    bias[...] = jnp.where(level_ref[...] > 0.5, 0.0, NEGATIVE)
    wo_copy.wait()
    for copy in copies:
        copy.wait()
    shift0 = mods_ref[0:1, :]
    scale0 = 1.0 + mods_ref[1:2, :]
    gate0 = mods_ref[2:3, :]
    scale1 = 1.0 + mods_ref[4:5, :]
    zero = jnp.zeros((1, D), F32)

    def norm_backward(dx, u, scale):
        factor, normed = norm_rows(u)
        shift_sum = jnp.sum(dx, axis=0, keepdims=True)
        scale_sum = jnp.sum(dx * normed, axis=0, keepdims=True)
        dn = dx * scale
        du = factor * (dn - normed * jnp.mean(dn * normed, axis=-1, keepdims=True))
        return du, shift_sum, scale_sum, jnp.sum(du, axis=0, keepdims=True)

    shift_sum, scale_sum, embed_sum, gate_sum = zero, zero, zero, zero
    for block in range(NBLK):
        rows = slice(block * BLK, (block + 1) * BLK)
        dx = dx_own_ref[rows, :].astype(F32) + dx_other_ref[rows, :].astype(F32)
        u = h1_ref[rows, :].astype(F32) + embeds_ref[1:2, :]
        du, a, b, c = norm_backward(dx, u, scale1)
        shift_sum, scale_sum, embed_sum = shift_sum + a, scale_sum + b, embed_sum + c
        g = g_ref[rows, :].astype(F32) + du
        gs[rows, :] = g
        gate_sum += jnp.sum(g * y0_ref[rows, :].astype(F32), axis=0, keepdims=True)
        dy = (g * gate0).astype(BF)
        dy_ref[rows, :] = dy
        do_ref[rows, :] = nt(dy, wo[...]).astype(BF)
        factor, normed = norm_rows(h_ref[rows, :].astype(F32) + embeds_ref[0:1, :])
        x_ref[rows, :] = (normed * scale0 + shift0).astype(BF)
    sums[2:3, :] = 0.5 * gate_sum
    sums[3:4, :] = 0.5 * shift_sum
    sums[4:5, :] = 0.5 * scale_sum
    sums[5:6, :] = gate1_ref[0:1, :]
    sums[7:8, :] = 0.5 * embed_sum
    attention_backward(
        q_ref, k_ref, v_ref, o_ref, do_ref, lse_ref, bias, dq_ref, dk_ref, dv_ref, dk_acc, dv_acc
    )
    shift_sum, scale_sum, embed_sum = zero, zero, zero
    for block in range(NBLK):
        rows = slice(block * BLK, (block + 1) * BLK)
        dx = unproject(rows, wq, wk, wv, dq_ref, dk_ref, dv_ref)
        dx0[rows, :] = dx
        u = h_ref[rows, :].astype(F32) + embeds_ref[0:1, :]
        du, a, b, c = norm_backward(dx, u, scale0)
        shift_sum, scale_sum, embed_sum = shift_sum + a, scale_sum + b, embed_sum + c
    sums[0:1, :] = shift_sum
    sums[1:2, :] = scale_sum
    sums[6:7, :] = embed_sum
    weight_grads(core, chip, x_ref, o_ref, dy_ref, dq_ref, dk_ref, dv_ref, grads)
    base = pl.multiple_of((chip % 4) * 32, 32)
    mine16 = pl.ds(pl.multiple_of(core * 16, 16), 16)
    other16 = pl.ds(pl.multiple_of((1 - core) * 16, 16), 16)
    chip_grads = grads.at[pl.ds(base, 32)]
    keep_ref[:, 0 : 5 * HALF] = (chip_grads[mine16, :] + grads1_ref[mine16, :]).astype(BF)
    send_ref[:, 0 : 5 * HALF] = (chip_grads[other16, :] + grads1_ref[other16, :]).astype(BF)
    total = jnp.concatenate([sums[...], jnp.zeros((8, D), F32)], axis=0).astype(BF)
    keep_ref[:, 5 * HALF : 7 * HALF] = total
    send_ref[:, 5 * HALF : 7 * HALF] = total
    first_half = core == 0
    chip_rows = dx0.at[pl.ds(pl.multiple_of(chip * 2 * CAP, 8), 2 * CAP)]
    lower = chip_rows[0:16, :]
    upper = chip_rows[CAP - 4 : 2 * CAP, :]
    upper = jnp.concatenate([upper[4:16], upper[0:4]], axis=0)
    keep_ref[:, 7 * HALF : 9 * HALF] = jnp.where(first_half, lower, upper).astype(BF)
    send_ref[:, 7 * HALF : 9 * HALF] = jnp.where(first_half, upper, lower).astype(BF)
    g_rows = gs.at[pl.ds(pl.multiple_of(chip * 2 * CAP, 8), 2 * CAP)]
    mine_ref[...] = jnp.where(first_half, g_rows[0:CAP, :], g_rows[CAP : 2 * CAP, :])


def third(ids, dx_own, dx_other, h1, h, g, level, y0, q, k, v, o, lse, grads1, gate1, embeds, mods, wq, wk, wv, wo):
    packed = sds((16, 9 * HALF), BF)
    half = pltpu.VMEM((SLOTS, HALF), BF)
    weight = pltpu.VMEM((D, HALF), BF)
    return call(
        third_kernel,
        (packed, packed, sds((CAP, D), F32)),
        [SSPEC] + [VSPEC] * 16 + [HSPEC] * 4,
        [
            weight, weight, weight, pltpu.VMEM((HALF, D), BF),
            pltpu.VMEM((SLOTS, D), BF), pltpu.VMEM((SLOTS, D), BF), half,
            half, half, half,
            pltpu.VMEM((SLOTS, DH), F32), pltpu.VMEM((SLOTS, DH), F32),
            pltpu.VMEM((DH, 5 * HALF), F32), pltpu.VMEM((SLOTS, 128), F32),
            pltpu.VMEM((SLOTS, D), F32), pltpu.VMEM((SLOTS, D), F32), pltpu.VMEM((8, D), F32),
            pltpu.SemaphoreType.DMA((4,)),
        ],
    )(ids, dx_own, dx_other, h1, h, g, level, y0, q, k, v, o, lse, grads1, gate1, embeds, mods, wq, wk, wv, wo)


def join_kernel(ids_ref, keep_ref, other_ref, out_ref):
    core = ids_ref[0]
    own_cols = pl.ds(pl.multiple_of(core * HALF, HALF), HALF)
    other_cols = pl.ds(pl.multiple_of((1 - core) * HALF, HALF), HALF)
    for part in range(3):
        rows = slice(16 * part, 16 * part + 16)
        cols = slice(part * HALF, (part + 1) * HALF)
        out_ref[rows, own_cols] = keep_ref[:, cols]
        out_ref[rows, other_cols] = other_ref[:, cols]
    both = keep_ref[:, 3 * HALF : 7 * HALF].astype(F32) + other_ref[:, 3 * HALF : 7 * HALF].astype(F32)
    both = both.astype(BF)
    out_ref[48:64, :] = both[:, 0:D]
    out_ref[64:80, :] = both[:, D : 2 * D]


def join(ids, keep, other):
    return call(join_kernel, sds((80, D), BF), [SSPEC, VSPEC, VSPEC])(ids, keep, other)


def hidden_kernel(keep_ref, other_ref, mine_ref, payload_ref, picker_ref, cot_ref, embeds_ref, mods_ref, out_ref):
    cols = slice(7 * HALF, 9 * HALF)
    dx = keep_ref[:, cols].astype(F32) + other_ref[:, cols].astype(F32)
    dx = dx[0:CAP]
    factor, normed = norm_rows(payload_ref[0:CAP, 0:D] + embeds_ref[0:1, :])
    dn = dx * (1.0 + mods_ref[1:2, :])
    du = factor * (dn - normed * jnp.mean(dn * normed, axis=-1, keepdims=True))
    rows = jnp.concatenate([mine_ref[...] + du, jnp.zeros((16 - CAP, D), F32)], axis=0).astype(BF)
    picker = picker_ref[...]
    placed = tn(picker, rows)
    taken = tn(picker, jnp.ones((16, 128), BF))
    taken = jnp.concatenate([taken] * 8, axis=1)
    out_ref[0] = jnp.where(taken > 0.5, placed.astype(BF), cot_ref[0])


def hidden_grad(keep, other, mine, payload, picker, cot, embeds, mods):
    return call(hidden_kernel, sds((1, TOK, D), BF), [VSPEC] * 8)(
        keep, other, mine, payload, picker, cot, embeds, mods
    )


def swap_cores(x):
    return lax.ppermute(x, "core", [(0, 1), (1, 0)])


def sequence_work(gathered, payload, picker, chip, cot, embeds, mods, weights):
    wq, wk, wv, wo = weights
    core = lax.axis_index("core")
    ids = jnp.stack([core, chip]).astype(jnp.int32)
    mods = mods.reshape(6, D)
    other = swap_cores(gathered)
    q, k, v, o, lse, h, g, level = first(ids, gathered, other, embeds, mods, wq, wk, wv)
    o_other = swap_cores(o)
    dx, h1, y0, grads1, gate1 = second(ids, o, o_other, h, g, level, embeds, mods, wq, wk, wv, wo)
    dx_other = swap_cores(dx)
    keep, send, mine = third(
        ids, dx, dx_other, h1, h, g, level, y0, q, k, v, o, lse, grads1, gate1, embeds, mods, wq, wk, wv, wo
    )
    received = swap_cores(send)
    joined = join(ids, keep, received)
    hidden = hidden_grad(keep, received, mine, payload, picker, cot, embeds, mods)
    return joined, hidden


def final_kernel(own_ref, other_ref, gq_ref, gk_ref, gv_ref, go_ref, embeds_ref, mods_ref):
    total = own_ref[...].astype(F32) + other_ref[...].astype(F32)
    gq_ref[...] = total[0:16]
    gk_ref[...] = total[16:32]
    gv_ref[...] = total[32:48]
    go_ref[...] = total[48:64]
    mods_ref[0] = total[64:67]
    mods_ref[1] = total[67:70]
    embeds_ref[...] = total[70:72]


def final(own, other):
    block = sds((16, D), F32)
    return call(
        final_kernel,
        (block, block, block, block, sds((2, D), F32), sds((2, 3, D), F32)),
        [VSPEC, VSPEC],
    )(own, other)


def dp_sum(joined):
    near = lax.ppermute(joined, "dp", [(i, i ^ 1) for i in range(4)])
    pair = (joined.astype(F32) + near.astype(F32)).astype(BF)
    far = lax.ppermute(pair, "dp", [(i, i ^ 2) for i in range(4)])
    return final(pair, far)


def shards(hidden, depth, cotangent, embeds, mods, w_query, w_key, w_value, w_out):
    payload, picker = pick(depth, hidden, cotangent)
    spread = jnp.broadcast_to(payload.astype(BF)[None], (CHIPS, 2 * CAP, WIDE))
    gathered = lax.all_to_all(spread, ("zl", "x", "y"), 0, 0, tiled=True)
    chip = (lax.axis_index("zl") * 4 + lax.axis_index("x")) * 4 + lax.axis_index("y")
    joined, grad_hidden = sequence_work(
        gathered, payload, picker, chip, cotangent, embeds, mods, (w_query, w_key, w_value, w_out)
    )
    gq, gk, gv, go, grad_embeds, grad_mods = dp_sum(joined)
    return (grad_hidden, gq, gk, gv, go, grad_embeds, grad_mods)


def solution(mesh):
    split = Mesh(mesh.devices.reshape(2, 4, 4, 2, 4), ("zl", "x", "y", "core", "dp"))
    ctx = ("zl", "x", "y", "core")
    in_specs = (P("dp", ctx, None), P("dp", ctx), P("dp", ctx, None)) + (P(),) * 6
    out_specs = (P("dp", ctx, None),) + (P(ctx, None),) * 4 + (P(), P())
    return jax.shard_map(shards, mesh=split, in_specs=in_specs, out_specs=out_specs, check_vma=False)
```

```python
import jax
import jax.numpy as jnp
from jax import lax
from jax.experimental import pallas as pl
from jax.experimental.pallas import tpu as pltpu
from jax.sharding import Mesh, PartitionSpec as P

D = 1024
H = 8
DH = 128
TOK = 128
CAP = 12
N_CTX = 64
CHIPS = 32
SLOTS = 768
HALF = 512
HEADS = 4
TILES = 24
PACKED = (TILES + 1) * 8
BLK = 256
NBLK = SLOTS // BLK
EPSILON = 1e-06
NEGATIVE = -1e30
EMPTY = 64.0
SCALE = DH ** (-0.5)
SCALE2 = SCALE * 1.4426950408889634
BF = jnp.bfloat16
F32 = jnp.float32

VSPEC = pl.BlockSpec(memory_space=pltpu.VMEM)


def nn(a, b):
    return lax.dot_general(a, b, (((1,), (0,)), ((), ())), preferred_element_type=F32)


def nt(a, b):
    return lax.dot_general(a, b, (((1,), (1,)), ((), ())), preferred_element_type=F32)


def tn(a, b):
    return lax.dot_general(a, b, (((0,), (0,)), ((), ())), preferred_element_type=F32)


def sds(shape, dtype):
    return jax.ShapeDtypeStruct(shape, dtype)


def call(kernel, out_shape, in_specs, scratch=(), vmem=16):
    single = not isinstance(out_shape, tuple)
    outs = (out_shape,) if single else out_shape
    shapes = tuple(pltpu.VMEM(s.shape, s.dtype) for s in outs)
    run = pl.pallas_call(
        kernel,
        out_shape=shapes[0] if single else shapes,
        in_specs=in_specs,
        out_specs=VSPEC if single else tuple(VSPEC for _ in outs),
        scratch_shapes=list(scratch),
        compiler_params=pltpu.CompilerParams(vmem_limit_bytes=vmem * 1024 * 1024),
    )

    def placed(*args):
        args = [
            pltpu.with_memory_space_constraint(a, pltpu.VMEM) if spec is VSPEC else a
            for a, spec in zip(args, in_specs)
        ]
        return run(*args)

    return placed


def pick_kernel(depth_ref, hidden_ref, cot_ref, payload_ref, picker_ref, rows_ref, both):
    depth = jnp.broadcast_to(depth_ref[...], (16, TOK))
    active = depth >= 2
    before = lax.broadcasted_iota(jnp.int32, (TOK, TOK), 0)
    upto = lax.broadcasted_iota(jnp.int32, (TOK, TOK), 1)
    upper = jnp.where(before <= upto, 1.0, 0.0).astype(BF)
    placing = nn(jnp.where(active, 1.0, 0.0).astype(BF), upper) - 1.0
    slot = lax.broadcasted_iota(jnp.int32, (16, TOK), 0)
    hit = active & (placing == slot.astype(F32)) & (slot < CAP)
    picker = jnp.where(hit, 1.0, 0.0)
    picker_ref[...] = picker.astype(BF)
    level = jnp.sum(picker * (depth - 1).astype(F32), axis=1, keepdims=True)
    rows = nn(picker.astype(BF), hidden_ref[0])
    both[0:CAP] = jnp.where(level > 0.5, rows, EMPTY)[0:CAP]
    both[CAP : 2 * CAP] = nn(picker.astype(BF), cot_ref[0])[0:CAP]
    lane = lax.broadcasted_iota(jnp.int32, (8, 128), 1)
    level = jnp.broadcast_to(level, (16, 128))
    tiles = [both[8 * r : 8 * r + 8, 128 * c : 128 * c + 128] for r in range(3) for c in range(8)]
    tiles.append(jnp.where(lane < 64, level[0:8], level[8:16]))
    payload_ref[...] = jnp.concatenate(tiles, axis=0).astype(BF)
    rows_ref[...] = both[0:16].astype(BF)


def pick(depth, hidden, cotangent):
    return call(
        pick_kernel,
        (sds((PACKED, 128), BF), sds((16, TOK), BF), sds((16, D), BF)),
        [VSPEC, VSPEC, VSPEC],
        [pltpu.VMEM((2 * CAP, D), F32)],
    )(depth, hidden, cotangent)


def causal_bias():
    key = lax.broadcasted_iota(jnp.int32, (BLK, BLK), 0)
    query = lax.broadcasted_iota(jnp.int32, (BLK, BLK), 1)
    return jnp.where(key <= query, 0.0, NEGATIVE).astype(F32)


def norm_rows(u):
    factor = lax.rsqrt(jnp.mean(u * u, axis=-1, keepdims=True) + EPSILON)
    return factor, u * factor


def biased_scores(k, q, bias_ref, causal, upto):
    s = nt(k, q)
    bias = bias_ref[0:upto, :]
    s = s + jnp.concatenate([bias, bias], axis=1)
    last = s[upto - BLK : upto] + causal
    if upto == BLK:
        return last
    return jnp.concatenate([s[: upto - BLK], last], axis=0)


def attention_forward(q_ref, k_ref, v_ref, o_ref, lse_ref, bias_ref):
    causal = causal_bias()

    def one_head(head, carry):
        cols = pl.ds(pl.multiple_of(head * DH, DH), DH)
        vt = v_ref[:, cols].T
        for block in range(NBLK):
            upto = (block + 1) * BLK
            rows = slice(block * BLK, upto)
            s = biased_scores(k_ref[0:upto, cols], q_ref[rows, cols], bias_ref, causal, upto)
            top = jnp.max(s, axis=0, keepdims=True)
            e = jnp.exp2((s - top) * SCALE2)
            total = jnp.sum(e, axis=0, keepdims=True)
            ot = nn(vt[:, 0:upto], e.astype(BF)) * (1.0 / total)
            o_ref[rows, cols] = ot.T.astype(BF)
            lse_ref[pl.ds(head, 1), rows] = jnp.maximum(top * SCALE2 + jnp.log2(total), -1e25)
        return carry

    lax.fori_loop(0, HEADS, one_head, 0)


def attention_backward(
    q_ref, k_ref, v_ref, o_ref, do_ref, lse_ref, bias_ref, dq_ref, dk_ref, dv_ref, dk_acc, dv_acc
):
    causal = causal_bias()

    def one_head(head, carry):
        cols = pl.ds(pl.multiple_of(head * DH, DH), DH)
        kt = k_ref[:, cols].T
        for block in range(NBLK - 1, -1, -1):
            upto = (block + 1) * BLK
            rows = slice(block * BLK, upto)
            q = q_ref[rows, cols]
            do = do_ref[rows, cols]
            inner = jnp.sum((do.astype(F32) * o_ref[rows, cols].astype(F32)).T, axis=0, keepdims=True)
            s = biased_scores(k_ref[0:upto, cols], q, bias_ref, causal, upto)
            p = jnp.exp2(s * SCALE2 - lse_ref[pl.ds(head, 1), rows])
            dp = nt(v_ref[0:upto, cols], do)
            ds = (p * (dp - inner)).astype(BF)
            dv_part = nn(p.astype(BF), do)
            dk_part = nn(ds, q)
            if block == NBLK - 1:
                dv_acc[...] = dv_part
                dk_acc[...] = dk_part
            else:
                dv_acc[0:upto] += dv_part
                dk_acc[0:upto] += dk_part
            dqt = nn(kt[:, 0:upto], ds)
            dq_ref[rows, cols] = (dqt.T * SCALE).astype(BF)
        dk_ref[:, cols] = (dk_acc[...] * SCALE).astype(BF)
        dv_ref[:, cols] = dv_acc[...].astype(BF)
        return carry

    lax.fori_loop(0, HEADS, one_head, 0)


def project(x, rows, wq, wk, wv, q_ref, k_ref, v_ref):
    q_ref[rows, :] = nn(x, wq[...]).astype(BF)
    k_ref[rows, :] = nn(x, wk[...]).astype(BF)
    v_ref[rows, :] = nn(x, wv[...]).astype(BF)


def unproject(rows, wq, wk, wv, dq_ref, dk_ref, dv_ref):
    return nt(dq_ref[rows, :], wq[...]) + nt(dk_ref[rows, :], wk[...]) + nt(dv_ref[rows, :], wv[...])


def place_block(block_ref, chip, base, start, hs, gs, level):
    tiles = block_ref[chip].astype(F32)
    rows_h = hs.at[pl.ds(base, 2 * CAP)]
    rows_g = gs.at[pl.ds(base, 2 * CAP)]
    rows_level = level.at[pl.ds(base, 2 * CAP)]
    for c in range(8):
        cols = slice(128 * c, 128 * c + 128)
        upper, middle, lower = (tiles[8 * (8 * r + c) : 8 * (8 * r + c) + 8] for r in range(3))
        rows_h[start : start + 8, cols] = upper
        rows_h[start + 8 : start + 12, cols] = middle[0:4]
        rows_g[start : start + 4, cols] = middle[4:8]
        rows_g[start + 4 : start + 12, cols] = lower
    depths = tiles[8 * TILES :]
    turned = pltpu.roll(depths, 64, 1)
    lane = lax.broadcasted_iota(jnp.int32, (8, 128), 1)
    rows_level[start : start + 8] = jnp.where(lane < 64, depths, turned)
    rows_level[start + 8 : start + 12] = jnp.where(lane < 64, turned, depths)[0:4]


def half_of(core, *weights):
    cols = pl.ds(pl.multiple_of(core * HALF, HALF), HALF)
    return [w.at[:, cols] for w in weights]


def weight_grads(core, chip, x_ref, o_ref, dy_ref, dq_ref, dk_ref, dv_ref, grads):
    strip = pl.multiple_of((chip // 4) * DH, DH)
    xs = x_ref[:, pl.ds(strip, DH)]
    grads[:, 0:HALF] = tn(xs, dq_ref[...])
    grads[:, HALF : 2 * HALF] = tn(xs, dk_ref[...])
    grads[:, 2 * HALF : 3 * HALF] = tn(xs, dv_ref[...])
    own = jnp.where(chip // 16 == core, 1.0, 0.0).astype(F32)
    o_strip = pl.multiple_of(((chip // 4) % 4) * DH, DH)
    os = o_ref[:, pl.ds(o_strip, DH)]
    grads[:, 3 * HALF :] = tn(os, dy_ref[...]) * own


def first_kernel(
    own_ref, other_ref, embeds_ref, mods_ref, wq_ref, wk_ref, wv_ref,
    q_ref, k_ref, v_ref, o_ref, lse_ref, h_ref, g_ref, level_ref,
    hs, gs, bias,
):
    core = lax.axis_index("core")
    wq, wk, wv = half_of(core, wq_ref, wk_ref, wv_ref)

    def place(even_ref, odd_ref):
        def one_chip(chip, carry):
            base = pl.multiple_of(chip * 2 * CAP, 8)
            place_block(even_ref, chip, base, 0, hs, gs, level_ref)
            place_block(odd_ref, chip, base, CAP, hs, gs, level_ref)
            return carry

        lax.fori_loop(0, CHIPS, one_chip, 0)

    @pl.when(core == 0)
    def _():
        place(own_ref, other_ref)

    @pl.when(core == 1)
    def _():
        place(other_ref, own_ref)

    bias[...] = jnp.where(level_ref[...] > 0.5, 0.0, NEGATIVE)
    g_ref[...] = gs[...].astype(BF)
    h_ref[...] = hs[...].astype(BF)
    embed = embeds_ref[0:1, :]
    shift = mods_ref[0, 0:1, :]
    scale = 1.0 + mods_ref[1, 0:1, :]
    for block in range(NBLK):
        rows = slice(block * BLK, (block + 1) * BLK)
        factor, normed = norm_rows(hs[rows, :] + embed)
        x = (normed * scale + shift).astype(BF)
        project(x, rows, wq, wk, wv, q_ref, k_ref, v_ref)
    attention_forward(q_ref, k_ref, v_ref, o_ref, lse_ref, bias)


def first(own, other, embeds, mods, wq, wk, wv):
    half = sds((SLOTS, HALF), BF)
    full = sds((SLOTS, D), BF)
    return call(
        first_kernel,
        (half, half, half, half, sds((8, SLOTS), F32), full, full, sds((SLOTS, 128), F32)),
        [VSPEC] * 7,
        [
            pltpu.VMEM((SLOTS, D), F32),
            pltpu.VMEM((SLOTS, D), F32),
            pltpu.VMEM((SLOTS, 128), F32),
        ],
        16,
    )(own, other, embeds, mods, wq, wk, wv)


def second_kernel(
    o_own_ref, o_other_ref, h_ref, g_ref, level_ref, embeds_ref, mods_ref,
    wq_ref, wk_ref, wv_ref, wo,
    dx_ref, h1_ref, y0_ref, grads_ref, gate_ref,
    x_ref, q_ref, k_ref, v_ref, o_ref, lse_ref, dy_ref, do_ref,
    dq_ref, dk_ref, dv_ref, dk_acc, dv_acc, grads, bias,
):
    core = lax.axis_index("core")
    chip = chip_index()
    wq, wk, wv = half_of(core, wq_ref, wk_ref, wv_ref)
    bias[...] = jnp.where(level_ref[...] > 1.5, 0.0, NEGATIVE)
    own_rows = pl.ds(pl.multiple_of(core * HALF, HALF), HALF)
    other_rows = pl.ds(pl.multiple_of((1 - core) * HALF, HALF), HALF)
    gate0 = mods_ref[2, 0:1, :]
    embed = embeds_ref[1:2, :]
    shift = mods_ref[0, 1:2, :]
    scale = 1.0 + mods_ref[1, 1:2, :]
    gate1 = mods_ref[2, 1:2, :]
    for block in range(NBLK):
        rows = slice(block * BLK, (block + 1) * BLK)
        y0 = nn(o_own_ref[rows, :], wo[own_rows, :]) + nn(o_other_ref[rows, :], wo[other_rows, :])
        y0_ref[rows, :] = y0.astype(BF)
        h1 = (h_ref[rows, :].astype(F32) + gate0 * y0).astype(BF)
        h1_ref[rows, :] = h1
        factor, normed = norm_rows(h1.astype(F32) + embed)
        x = (normed * scale + shift).astype(BF)
        x_ref[rows, :] = x
        project(x, rows, wq, wk, wv, q_ref, k_ref, v_ref)
        deep = jnp.where(level_ref[rows, 0:1] > 1.5, 1.0, 0.0)
        dy = (g_ref[rows, :].astype(F32) * deep * gate1).astype(BF)
        dy_ref[rows, :] = dy
        do_ref[rows, :] = nt(dy, wo[own_rows, :]).astype(BF)
    attention_forward(q_ref, k_ref, v_ref, o_ref, lse_ref, bias)
    attention_backward(
        q_ref, k_ref, v_ref, o_ref, do_ref, lse_ref, bias, dq_ref, dk_ref, dv_ref, dk_acc, dv_acc
    )
    gate_sum = jnp.zeros((1, D), F32)
    for block in range(NBLK):
        rows = slice(block * BLK, (block + 1) * BLK)
        dx_ref[rows, :] = unproject(rows, wq, wk, wv, dq_ref, dk_ref, dv_ref).astype(BF)
        y1 = nn(o_ref[rows, :], wo[own_rows, :])
        deep = jnp.where(level_ref[rows, 0:1] > 1.5, 1.0, 0.0)
        gate_sum += jnp.sum(g_ref[rows, :].astype(F32) * deep * y1, axis=0, keepdims=True)
    gate_ref[...] = jnp.broadcast_to(gate_sum, (8, D))
    weight_grads(core, chip, x_ref, o_ref, dy_ref, dq_ref, dk_ref, dv_ref, grads)
    grads_ref[...] = grads[pl.ds(pl.multiple_of((chip % 4) * 32, 32), 32), :]


def second(o_own, o_other, h, g, level, embeds, mods, wq, wk, wv, wo):
    full = sds((SLOTS, D), BF)
    half = pltpu.VMEM((SLOTS, HALF), BF)
    return call(
        second_kernel,
        (full, full, full, sds((32, 5 * HALF), F32), sds((8, D), F32)),
        [VSPEC] * 11,
        [
            pltpu.VMEM((SLOTS, D), BF), half, half, half, half,
            pltpu.VMEM((8, SLOTS), F32), pltpu.VMEM((SLOTS, D), BF), half,
            half, half, half,
            pltpu.VMEM((SLOTS, DH), F32), pltpu.VMEM((SLOTS, DH), F32),
            pltpu.VMEM((DH, 5 * HALF), F32), pltpu.VMEM((SLOTS, 128), F32),
        ],
        22,
    )(o_own, o_other, h, g, level, embeds, mods, wq, wk, wv, wo)


def third_kernel(
    dx_own_ref, dx_other_ref, h1_ref, h_ref, g_ref, level_ref, y0_ref,
    q_ref, k_ref, v_ref, o_ref, lse_ref, grads1_ref, gate1_ref, embeds_ref, mods_ref,
    wq_ref, wk_ref, wv_ref, wo_ref,
    keep_ref, send_ref, mine_ref,
    x_ref, dy_ref, do_ref, dq_ref, dk_ref, dv_ref, dk_acc, dv_acc, grads,
    bias, gs, dx0, sums,
):
    core = lax.axis_index("core")
    chip = chip_index()
    wq, wk, wv = half_of(core, wq_ref, wk_ref, wv_ref)
    wo = wo_ref.at[pl.ds(pl.multiple_of(core * HALF, HALF), HALF)]
    bias[...] = jnp.where(level_ref[...] > 0.5, 0.0, NEGATIVE)
    shift0 = mods_ref[0, 0:1, :]
    scale0 = 1.0 + mods_ref[1, 0:1, :]
    gate0 = mods_ref[2, 0:1, :]
    scale1 = 1.0 + mods_ref[1, 1:2, :]
    zero = jnp.zeros((1, D), F32)

    def norm_backward(dx, u, scale):
        factor, normed = norm_rows(u)
        shift_sum = jnp.sum(dx, axis=0, keepdims=True)
        scale_sum = jnp.sum(dx * normed, axis=0, keepdims=True)
        dn = dx * scale
        du = factor * (dn - normed * jnp.mean(dn * normed, axis=-1, keepdims=True))
        return du, shift_sum, scale_sum, jnp.sum(du, axis=0, keepdims=True)

    shift_sum, scale_sum, embed_sum, gate_sum = zero, zero, zero, zero
    for block in range(NBLK):
        rows = slice(block * BLK, (block + 1) * BLK)
        dx = dx_own_ref[rows, :].astype(F32) + dx_other_ref[rows, :].astype(F32)
        u = h1_ref[rows, :].astype(F32) + embeds_ref[1:2, :]
        du, a, b, c = norm_backward(dx, u, scale1)
        shift_sum, scale_sum, embed_sum = shift_sum + a, scale_sum + b, embed_sum + c
        g = g_ref[rows, :].astype(F32) + du
        gs[rows, :] = g
        gate_sum += jnp.sum(g * y0_ref[rows, :].astype(F32), axis=0, keepdims=True)
        dy = (g * gate0).astype(BF)
        dy_ref[rows, :] = dy
        do_ref[rows, :] = nt(dy, wo[...]).astype(BF)
        factor, normed = norm_rows(h_ref[rows, :].astype(F32) + embeds_ref[0:1, :])
        x_ref[rows, :] = (normed * scale0 + shift0).astype(BF)
    sums[2:3, :] = 0.5 * gate_sum
    sums[3:4, :] = 0.5 * shift_sum
    sums[4:5, :] = 0.5 * scale_sum
    sums[5:6, :] = gate1_ref[0:1, :]
    sums[7:8, :] = 0.5 * embed_sum
    attention_backward(
        q_ref, k_ref, v_ref, o_ref, do_ref, lse_ref, bias, dq_ref, dk_ref, dv_ref, dk_acc, dv_acc
    )
    shift_sum, scale_sum, embed_sum = zero, zero, zero
    for block in range(NBLK):
        rows = slice(block * BLK, (block + 1) * BLK)
        dx = unproject(rows, wq, wk, wv, dq_ref, dk_ref, dv_ref)
        dx0[rows, :] = dx
        u = h_ref[rows, :].astype(F32) + embeds_ref[0:1, :]
        du, a, b, c = norm_backward(dx, u, scale0)
        shift_sum, scale_sum, embed_sum = shift_sum + a, scale_sum + b, embed_sum + c
    sums[0:1, :] = shift_sum
    sums[1:2, :] = scale_sum
    sums[6:7, :] = embed_sum
    weight_grads(core, chip, x_ref, o_ref, dy_ref, dq_ref, dk_ref, dv_ref, grads)
    base = pl.multiple_of((chip % 4) * 32, 32)
    mine16 = pl.ds(pl.multiple_of(core * 16, 16), 16)
    other16 = pl.ds(pl.multiple_of((1 - core) * 16, 16), 16)
    chip_grads = grads.at[pl.ds(base, 32)]
    keep_ref[:, 0 : 5 * HALF] = (chip_grads[mine16, :] + grads1_ref[mine16, :]).astype(BF)
    send_ref[:, 0 : 5 * HALF] = (chip_grads[other16, :] + grads1_ref[other16, :]).astype(BF)
    total = jnp.concatenate([sums[...], jnp.zeros((8, D), F32)], axis=0).astype(BF)
    keep_ref[:, 5 * HALF : 7 * HALF] = total
    send_ref[:, 5 * HALF : 7 * HALF] = total
    first_half = core == 0
    chip_rows = dx0.at[pl.ds(pl.multiple_of(chip * 2 * CAP, 8), 2 * CAP)]
    lower = chip_rows[0:16, :]
    upper = chip_rows[CAP - 4 : 2 * CAP, :]
    upper = jnp.concatenate([upper[4:16], upper[0:4]], axis=0)
    keep_ref[:, 7 * HALF : 9 * HALF] = jnp.where(first_half, lower, upper).astype(BF)
    send_ref[:, 7 * HALF : 9 * HALF] = jnp.where(first_half, upper, lower).astype(BF)
    g_rows = gs.at[pl.ds(pl.multiple_of(chip * 2 * CAP, 8), 2 * CAP)]
    mine_ref[...] = jnp.where(first_half, g_rows[0:CAP, :], g_rows[CAP : 2 * CAP, :])


def third(dx_own, dx_other, h1, h, g, level, y0, q, k, v, o, lse, grads1, gate1, embeds, mods, wq, wk, wv, wo):
    packed = sds((16, 9 * HALF), BF)
    half = pltpu.VMEM((SLOTS, HALF), BF)
    return call(
        third_kernel,
        (packed, packed, sds((CAP, D), F32)),
        [VSPEC] * 20,
        [
            pltpu.VMEM((SLOTS, D), BF), pltpu.VMEM((SLOTS, D), BF), half,
            half, half, half,
            pltpu.VMEM((SLOTS, DH), F32), pltpu.VMEM((SLOTS, DH), F32),
            pltpu.VMEM((DH, 5 * HALF), F32), pltpu.VMEM((SLOTS, 128), F32),
            pltpu.VMEM((SLOTS, D), F32), pltpu.VMEM((SLOTS, D), F32), pltpu.VMEM((8, D), F32),
        ],
        26,
    )(dx_own, dx_other, h1, h, g, level, y0, q, k, v, o, lse, grads1, gate1, embeds, mods, wq, wk, wv, wo)


def join_kernel(keep_ref, other_ref, out_ref):
    core = lax.axis_index("core")
    own_cols = pl.ds(pl.multiple_of(core * HALF, HALF), HALF)
    other_cols = pl.ds(pl.multiple_of((1 - core) * HALF, HALF), HALF)
    for part in range(3):
        rows = slice(16 * part, 16 * part + 16)
        cols = slice(part * HALF, (part + 1) * HALF)
        out_ref[rows, own_cols] = keep_ref[:, cols]
        out_ref[rows, other_cols] = other_ref[:, cols]
    both = keep_ref[:, 3 * HALF : 7 * HALF].astype(F32) + other_ref[:, 3 * HALF : 7 * HALF].astype(F32)
    both = both.astype(BF)
    out_ref[48:64, :] = both[:, 0:D]
    out_ref[64:80, :] = both[:, D : 2 * D]


def join(keep, other):
    return call(join_kernel, sds((80, D), BF), [VSPEC, VSPEC])(keep, other)


def hidden_kernel(keep_ref, other_ref, mine_ref, rows_ref, picker_ref, cot_ref, embeds_ref, mods_ref, out_ref):
    cols = slice(7 * HALF, 9 * HALF)
    dx = keep_ref[:, cols].astype(F32) + other_ref[:, cols].astype(F32)
    dx = dx[0:CAP]
    factor, normed = norm_rows(rows_ref[...].astype(F32)[0:CAP] + embeds_ref[0:1, :])
    dn = dx * (1.0 + mods_ref[1, 0:1, :])
    du = factor * (dn - normed * jnp.mean(dn * normed, axis=-1, keepdims=True))
    rows = jnp.concatenate([mine_ref[...] + du, jnp.zeros((16 - CAP, D), F32)], axis=0).astype(BF)
    picker = picker_ref[...]
    placed = tn(picker, rows)
    taken = tn(picker, jnp.ones((16, 128), BF))
    taken = jnp.concatenate([taken] * 8, axis=1)
    out_ref[0] = jnp.where(taken > 0.5, placed.astype(BF), cot_ref[0])


def hidden_grad(keep, other, mine, rows, picker, cot, embeds, mods):
    return call(hidden_kernel, sds((1, TOK, D), BF), [VSPEC] * 8)(
        keep, other, mine, rows, picker, cot, embeds, mods
    )


def swap_cores(x):
    return lax.ppermute(x, "core", [(0, 1), (1, 0)])


def chip_index():
    return (lax.axis_index("zl") * 4 + lax.axis_index("x")) * 4 + lax.axis_index("y")


def sequence_work(gathered, rows, picker, cot, embeds, mods, weights):
    wq, wk, wv, wo = weights
    mods = mods.transpose(1, 0, 2)
    other = swap_cores(gathered)
    q, k, v, o, lse, h, g, level = first(gathered, other, embeds, mods, wq, wk, wv)
    o_other = swap_cores(o)
    dx, h1, y0, grads1, gate1 = second(o, o_other, h, g, level, embeds, mods, wq, wk, wv, wo)
    dx_other = swap_cores(dx)
    keep, send, mine = third(
        dx, dx_other, h1, h, g, level, y0, q, k, v, o, lse, grads1, gate1, embeds, mods, wq, wk, wv, wo
    )
    received = swap_cores(send)
    joined = join(keep, received)
    hidden = hidden_grad(keep, received, mine, rows, picker, cot, embeds, mods)
    return joined, hidden


def final_kernel(own_ref, other_ref, gq_ref, gk_ref, gv_ref, go_ref, embeds_ref, mods_ref):
    total = own_ref[...].astype(F32) + other_ref[...].astype(F32)
    gq_ref[...] = total[0:16]
    gk_ref[...] = total[16:32]
    gv_ref[...] = total[32:48]
    go_ref[...] = total[48:64]
    for kind in range(3):
        for section in range(2):
            row = 64 + 3 * section + kind
            mods_ref[kind, section : section + 1, :] = total[row : row + 1]
    embeds_ref[...] = total[70:72]


def final(own, other):
    block = sds((16, D), F32)
    return call(
        final_kernel,
        (block, block, block, block, sds((2, D), F32), sds((3, 2, D), F32)),
        [VSPEC, VSPEC],
    )(own, other)


def dp_sum(joined):
    near = lax.ppermute(joined, "dp", [(i, i ^ 1) for i in range(4)])
    pair = (joined.astype(F32) + near.astype(F32)).astype(BF)
    far = lax.ppermute(pair, "dp", [(i, i ^ 2) for i in range(4)])
    return final(pair, far)


def shards(hidden, depth, cotangent, embeds, mods, w_query, w_key, w_value, w_out):
    payload, picker, rows = pick(depth, hidden, cotangent)
    spread = jnp.broadcast_to(payload[None], (CHIPS, PACKED, 128))
    gathered = lax.all_to_all(spread, ("zl", "x", "y"), 0, 0, tiled=True)
    joined, grad_hidden = sequence_work(
        gathered, rows, picker, cotangent, embeds, mods, (w_query, w_key, w_value, w_out)
    )
    gq, gk, gv, go, grad_embeds, grad_mods = dp_sum(joined)
    return (grad_hidden, gq, gk, gv, go, grad_embeds, grad_mods.transpose(1, 0, 2))


def solution(mesh):
    split = Mesh(mesh.devices.reshape(2, 4, 4, 2, 4), ("zl", "x", "y", "core", "dp"))
    ctx = ("zl", "x", "y", "core")
    in_specs = (P("dp", ctx, None), P("dp", ctx), P("dp", ctx, None)) + (P(),) * 6
    out_specs = (P("dp", ctx, None),) + (P(ctx, None),) * 4 + (P(), P())
    return jax.shard_map(shards, mesh=split, in_specs=in_specs, out_specs=out_specs, check_vma=False)
```

```python
import jax
import jax.numpy as jnp
from jax import lax
from jax.experimental import pallas as pl
from jax.experimental.pallas import tpu as pltpu
from jax.sharding import Mesh, PartitionSpec as P

D = 1024
H = 8
DH = 128
TOK = 128
CAP = 12
N_CTX = 64
CHIPS = 32
SLOTS = 768
HALF = 512
HEADS = 4
FORWARD_HEADS = 4
BACKWARD_HEADS = 4
TILES = 24
PACKED = (TILES + 1) * 8
BLK = 256
NBLK = SLOTS // BLK
EPSILON = 1e-06
NEGATIVE = -1e30
EMPTY = 64.0
SCALE = DH ** (-0.5)
SCALE2 = SCALE * 1.4426950408889634
BF = jnp.bfloat16
F32 = jnp.float32

VSPEC = pl.BlockSpec(memory_space=pltpu.VMEM)
LOAD = pl.BlockSpec(memory_space=pltpu.VMEM)
HSPEC = pl.BlockSpec(memory_space=pl.ANY)


def nn(a, b):
    return lax.dot_general(a, b, (((1,), (0,)), ((), ())), preferred_element_type=F32)


def nt(a, b):
    return lax.dot_general(a, b, (((1,), (1,)), ((), ())), preferred_element_type=F32)


def tn(a, b):
    return lax.dot_general(a, b, (((0,), (0,)), ((), ())), preferred_element_type=F32)


def sds(shape, dtype):
    return jax.ShapeDtypeStruct(shape, dtype)


def call(kernel, outs, in_specs, scratch=(), vmem=16, pinned=True):
    if pinned:
        outs = tuple(pltpu.VMEM(s.shape, s.dtype) for s in outs)
    run = pl.pallas_call(
        kernel,
        out_shape=outs,
        in_specs=in_specs,
        out_specs=tuple(VSPEC for _ in outs),
        scratch_shapes=list(scratch),
        compiler_params=pltpu.CompilerParams(vmem_limit_bytes=vmem * 1024 * 1024),
    )

    def placed(*args):
        spaces = [pltpu.VMEM if spec is VSPEC else pltpu.HBM for spec in in_specs]
        return run(*(pltpu.with_memory_space_constraint(a, m) for a, m in zip(args, spaces)))

    return placed


def pick_kernel(depth_ref, hidden_ref, cot_ref, payload_ref, picker_ref, rows_ref, both):
    depth = jnp.broadcast_to(depth_ref[...], (16, TOK))
    active = depth >= 2
    before = lax.broadcasted_iota(jnp.int32, (TOK, TOK), 0)
    upto = lax.broadcasted_iota(jnp.int32, (TOK, TOK), 1)
    upper = jnp.where(before <= upto, 1.0, 0.0).astype(BF)
    placing = nn(jnp.where(active, 1.0, 0.0).astype(BF), upper) - 1.0
    slot = lax.broadcasted_iota(jnp.int32, (16, TOK), 0)
    hit = active & (placing == slot.astype(F32)) & (slot < CAP)
    picker = jnp.where(hit, 1.0, 0.0)
    picker_ref[...] = picker.astype(BF)
    level = jnp.sum(picker * (depth - 1).astype(F32), axis=1, keepdims=True)
    rows = nn(picker.astype(BF), hidden_ref[0])
    both[0:CAP] = jnp.where(level > 0.5, rows, EMPTY)[0:CAP]
    both[CAP : 2 * CAP] = nn(picker.astype(BF), cot_ref[0])[0:CAP]
    lane = lax.broadcasted_iota(jnp.int32, (8, 128), 1)
    level = jnp.broadcast_to(level, (16, 128))
    tiles = [both[8 * r : 8 * r + 8, 128 * c : 128 * c + 128] for r in range(3) for c in range(8)]
    tiles.append(jnp.where(lane < 64, level[0:8], level[8:16]))
    payload_ref[...] = jnp.concatenate(tiles, axis=0).astype(BF)
    rows_ref[...] = both[0:16].astype(BF)


def pick(depth, hidden, cotangent):
    return call(
        pick_kernel,
        (sds((PACKED, 128), BF), sds((16, TOK), BF), sds((16, D), BF)),
        [LOAD, LOAD, LOAD],
        [pltpu.VMEM((2 * CAP, D), F32)],
    )(depth, hidden, cotangent)


def causal_bias():
    key = lax.broadcasted_iota(jnp.int32, (BLK, BLK), 0)
    query = lax.broadcasted_iota(jnp.int32, (BLK, BLK), 1)
    return jnp.where(key <= query, 0.0, NEGATIVE).astype(F32)


def norm_rows(u):
    factor = lax.rsqrt(jnp.mean(u * u, axis=-1, keepdims=True) + EPSILON)
    return factor, u * factor


def biased_scores(k, q, bias_ref, causal, upto):
    s = nt(k, q)
    bias = bias_ref[0:upto, :]
    s = s + jnp.concatenate([bias, bias], axis=1)
    last = s[upto - BLK : upto] + causal
    if upto == BLK:
        return last
    return jnp.concatenate([s[: upto - BLK], last], axis=0)


def head_cols(head):
    return pl.ds(pl.multiple_of(head * DH, DH), DH)


def attention_forward(q_ref, k_ref, v_ref, o_ref, lse_ref, bias_ref):
    causal = causal_bias()
    ones = jnp.ones((16, SLOTS), BF)

    def some_heads(step, carry):
        items = []
        for part in range(FORWARD_HEADS):
            head = step * FORWARD_HEADS + part
            cols = head_cols(head)
            vt = jnp.concatenate([v_ref[:, cols].T, ones], axis=0)
            items += [(head, cols, vt, block) for block in range(NBLK)]

        def start(head, cols, vt, block):
            upto = (block + 1) * BLK
            s = biased_scores(k_ref[0:upto, cols], q_ref[block * BLK : upto, cols], bias_ref, causal, upto)
            return s, jnp.max(s, axis=0, keepdims=True)

        def finish(head, cols, vt, block, s, top):
            upto = (block + 1) * BLK
            rows = slice(block * BLK, upto)
            e = jnp.exp2((s - top) * SCALE2).astype(BF)
            both = nn(vt[:, 0:upto], e)
            total = both[DH : DH + 1]
            o_ref[rows, cols] = (both[0:DH] * (1.0 / total)).T.astype(BF)
            lse_ref[pl.ds(head, 1), rows] = jnp.maximum(top * SCALE2 + jnp.log2(total), -1e25)

        state = start(*items[0])
        for i, item in enumerate(items):
            following = start(*items[i + 1]) if i + 1 < len(items) else None
            finish(*item, *state)
            state = following
        return carry

    lax.fori_loop(0, HEADS // FORWARD_HEADS, some_heads, 0)


def attention_backward(
    q_ref, k_ref, v_ref, o_ref, do_ref, lse_ref, bias_ref, dq_ref, dk_ref, dv_ref, ps, dss
):
    causal = causal_bias()

    def some_heads(step, carry):
        items = []
        for part in range(BACKWARD_HEADS):
            head = step * BACKWARD_HEADS + part
            cols = head_cols(head)
            kt = k_ref[:, cols].T
            items += [(head, part % 2, cols, kt, block) for block in range(NBLK)]

        def start(head, slot, cols, kt, block):
            upto = (block + 1) * BLK
            rows = slice(block * BLK, upto)
            s = biased_scores(k_ref[0:upto, cols], q_ref[rows, cols], bias_ref, causal, upto)
            return s, nt(v_ref[0:upto, cols], do_ref[rows, cols])

        def finish(head, slot, cols, kt, block, s, dp):
            upto = (block + 1) * BLK
            rows = slice(block * BLK, upto)
            product = do_ref[rows, cols].astype(F32) * o_ref[rows, cols].astype(F32)
            inner = jnp.sum(product.T, axis=0, keepdims=True)
            p = jnp.exp2(s * SCALE2 - lse_ref[pl.ds(head, 1), rows])
            ds = (p * (dp - inner)).astype(BF)
            ps[slot, 0:upto, rows] = p.astype(BF)
            dss[slot, 0:upto, rows] = ds
            dq_ref[rows, cols] = (nn(kt[:, 0:upto], ds).T * SCALE).astype(BF)

        def close(head, slot, cols):
            for block in range(NBLK):
                rows = slice(block * BLK, (block + 1) * BLK)
                later = slice(block * BLK, SLOTS)
                dv_ref[rows, cols] = nn(ps[slot, rows, later], do_ref[later, cols]).astype(BF)
                dk_ref[rows, cols] = (nn(dss[slot, rows, later], q_ref[later, cols]) * SCALE).astype(BF)

        state = start(*items[0])
        for i, item in enumerate(items):
            following = start(*items[i + 1]) if i + 1 < len(items) else None
            finish(*item, *state)
            state = following
            if item[-1] == NBLK - 1:
                close(*item[:3])
        return carry

    lax.fori_loop(0, HEADS // BACKWARD_HEADS, some_heads, 0)


def project(x, rows, wq, wk, wv, q_ref, k_ref, v_ref):
    q_ref[rows, :] = nn(x, wq[...]).astype(BF)
    k_ref[rows, :] = nn(x, wk[...]).astype(BF)
    v_ref[rows, :] = nn(x, wv[...]).astype(BF)


def unproject(rows, wq, wk, wv, dq_ref, dk_ref, dv_ref):
    return nt(dq_ref[rows, :], wq[...]) + nt(dk_ref[rows, :], wk[...]) + nt(dv_ref[rows, :], wv[...])


def place_block(block_ref, chip, base, start, hs, gs, level):
    tiles = block_ref[chip].astype(F32)
    rows_h = hs.at[pl.ds(base, 2 * CAP)]
    rows_g = gs.at[pl.ds(base, 2 * CAP)]
    rows_level = level.at[pl.ds(base, 2 * CAP)]
    for c in range(8):
        cols = slice(128 * c, 128 * c + 128)
        upper, middle, lower = (tiles[8 * (8 * r + c) : 8 * (8 * r + c) + 8] for r in range(3))
        rows_h[start : start + 8, cols] = upper
        rows_h[start + 8 : start + 12, cols] = middle[0:4]
        rows_g[start : start + 4, cols] = middle[4:8]
        rows_g[start + 4 : start + 12, cols] = lower
    depths = tiles[8 * TILES :]
    turned = pltpu.roll(depths, 64, 1)
    lane = lax.broadcasted_iota(jnp.int32, (8, 128), 1)
    rows_level[start : start + 8] = jnp.where(lane < 64, depths, turned)
    rows_level[start + 8 : start + 12] = jnp.where(lane < 64, turned, depths)[0:4]


def weight_grads(core, chip, x_ref, o_ref, dy_ref, dq_ref, dk_ref, dv_ref, grads):
    strip = pl.multiple_of((chip // 4) * DH, DH)
    xs = x_ref[:, pl.ds(strip, DH)]
    grads[:, 0:HALF] = tn(xs, dq_ref[...])
    grads[:, HALF : 2 * HALF] = tn(xs, dk_ref[...])
    grads[:, 2 * HALF : 3 * HALF] = tn(xs, dv_ref[...])
    own = jnp.where(chip // 16 == core, 1.0, 0.0).astype(F32)
    o_strip = pl.multiple_of(((chip // 4) % 4) * DH, DH)
    os = o_ref[:, pl.ds(o_strip, DH)]
    grads[:, 3 * HALF :] = tn(os, dy_ref[...]) * own


def first_kernel(
    own_ref, other_ref, embeds_ref, mods_ref, wq_hbm, wk_hbm, wv_hbm, wo_hbm,
    q_ref, k_ref, v_ref, o_ref, lse_ref, h_ref, g_ref, level_ref, wq, wk, wv, wo,
    hs, gs, bias, sems,
):
    core = lax.axis_index("core")
    half = pl.ds(pl.multiple_of(core * HALF, HALF), HALF)
    copies = [
        pltpu.make_async_copy(source.at[:, half], target, sems.at[i])
        for i, (source, target) in enumerate(((wq_hbm, wq), (wk_hbm, wk), (wv_hbm, wv)))
    ]
    copies.append(pltpu.make_async_copy(wo_hbm, wo, sems.at[3]))
    for copy in copies:
        copy.start()

    def place(even_ref, odd_ref):
        def one_chip(chip, carry):
            base = pl.multiple_of(chip * 2 * CAP, 8)
            place_block(even_ref, chip, base, 0, hs, gs, level_ref)
            place_block(odd_ref, chip, base, CAP, hs, gs, level_ref)
            return carry

        lax.fori_loop(0, CHIPS, one_chip, 0)

    @pl.when(core == 0)
    def _():
        place(own_ref, other_ref)

    @pl.when(core == 1)
    def _():
        place(other_ref, own_ref)

    bias[...] = jnp.where(level_ref[...] > 0.5, 0.0, NEGATIVE)
    g_ref[...] = gs[...].astype(BF)
    h_ref[...] = hs[...].astype(BF)
    for copy in copies:
        copy.wait()
    embed = embeds_ref[0:1, :]
    shift = mods_ref[0, 0:1, :]
    scale = 1.0 + mods_ref[1, 0:1, :]
    for block in range(NBLK):
        rows = slice(block * BLK, (block + 1) * BLK)
        factor, normed = norm_rows(hs[rows, :] + embed)
        x = (normed * scale + shift).astype(BF)
        project(x, rows, wq, wk, wv, q_ref, k_ref, v_ref)
    attention_forward(q_ref, k_ref, v_ref, o_ref, lse_ref, bias)


def first(own, other, embeds, mods, wq, wk, wv, wo):
    half = sds((SLOTS, HALF), BF)
    full = sds((SLOTS, D), BF)
    return call(
        first_kernel,
        (half, half, half, half, sds((8, SLOTS), F32), full, full, sds((SLOTS, 128), F32))
        + (sds((D, HALF), BF),) * 3
        + (sds((D, D), BF),),
        [VSPEC] * 4 + [HSPEC] * 4,
        [
            pltpu.VMEM((SLOTS, D), F32),
            pltpu.VMEM((SLOTS, D), F32),
            pltpu.VMEM((SLOTS, 128), F32),
            pltpu.SemaphoreType.DMA((4,)),
        ],
        16,
    )(own, other, embeds, mods, wq, wk, wv, wo)


def second_kernel(
    o_own_ref, o_other_ref, h_ref, g_ref, level_ref, embeds_ref, mods_ref,
    wq, wk, wv, wo,
    dx_ref, h1_ref, y0_ref, grads_ref, gate_ref,
    x_ref, q_ref, k_ref, v_ref, o_ref, lse_ref, dy_ref, do_ref,
    dq_ref, dk_ref, dv_ref, ps, dss, grads, bias,
):
    core = lax.axis_index("core")
    chip = chip_index()
    bias[...] = jnp.where(level_ref[...] > 1.5, 0.0, NEGATIVE)
    own_rows = pl.ds(pl.multiple_of(core * HALF, HALF), HALF)
    other_rows = pl.ds(pl.multiple_of((1 - core) * HALF, HALF), HALF)
    gate0 = mods_ref[2, 0:1, :]
    embed = embeds_ref[1:2, :]
    shift = mods_ref[0, 1:2, :]
    scale = 1.0 + mods_ref[1, 1:2, :]
    gate1 = mods_ref[2, 1:2, :]
    for block in range(NBLK):
        rows = slice(block * BLK, (block + 1) * BLK)
        y0 = nn(o_own_ref[rows, :], wo[own_rows, :]) + nn(o_other_ref[rows, :], wo[other_rows, :])
        y0_ref[rows, :] = y0.astype(BF)
        h1 = (h_ref[rows, :].astype(F32) + gate0 * y0).astype(BF)
        h1_ref[rows, :] = h1
        factor, normed = norm_rows(h1.astype(F32) + embed)
        x = (normed * scale + shift).astype(BF)
        x_ref[rows, :] = x
        project(x, rows, wq, wk, wv, q_ref, k_ref, v_ref)
        deep = jnp.where(level_ref[rows, 0:1] > 1.5, 1.0, 0.0)
        dy = (g_ref[rows, :].astype(F32) * deep * gate1).astype(BF)
        dy_ref[rows, :] = dy
        do_ref[rows, :] = nt(dy, wo[own_rows, :]).astype(BF)
    attention_forward(q_ref, k_ref, v_ref, o_ref, lse_ref, bias)
    attention_backward(
        q_ref, k_ref, v_ref, o_ref, do_ref, lse_ref, bias, dq_ref, dk_ref, dv_ref, ps, dss
    )
    gate_sum = jnp.zeros((1, D), F32)
    for block in range(NBLK):
        rows = slice(block * BLK, (block + 1) * BLK)
        dx_ref[rows, :] = unproject(rows, wq, wk, wv, dq_ref, dk_ref, dv_ref).astype(BF)
        y1 = nn(o_ref[rows, :], wo[own_rows, :])
        deep = jnp.where(level_ref[rows, 0:1] > 1.5, 1.0, 0.0)
        gate_sum += jnp.sum(g_ref[rows, :].astype(F32) * deep * y1, axis=0, keepdims=True)
    gate_ref[...] = jnp.broadcast_to(gate_sum, (8, D))
    weight_grads(core, chip, x_ref, o_ref, dy_ref, dq_ref, dk_ref, dv_ref, grads)
    grads_ref[...] = grads[pl.ds(pl.multiple_of((chip % 4) * 32, 32), 32), :]


def second(o_own, o_other, h, g, level, embeds, mods, wq, wk, wv, wo):
    full = sds((SLOTS, D), BF)
    half = pltpu.VMEM((SLOTS, HALF), BF)
    return call(
        second_kernel,
        (full, full, full, sds((32, 5 * HALF), F32), sds((8, D), F32)),
        [VSPEC] * 11,
        [
            pltpu.VMEM((SLOTS, D), BF), half, half, half, half,
            pltpu.VMEM((8, SLOTS), F32), pltpu.VMEM((SLOTS, D), BF), half,
            half, half, half,
            pltpu.VMEM((2, SLOTS, SLOTS), BF), pltpu.VMEM((2, SLOTS, SLOTS), BF),
            pltpu.VMEM((DH, 5 * HALF), F32), pltpu.VMEM((SLOTS, 128), F32),
        ],
        28,
    )(o_own, o_other, h, g, level, embeds, mods, wq, wk, wv, wo)


def third_kernel(
    dx_own_ref, dx_other_ref, h1_ref, h_ref, g_ref, level_ref, y0_ref,
    q_ref, k_ref, v_ref, o_ref, lse_ref, grads1_ref, gate1_ref, embeds_ref, mods_ref,
    wq, wk, wv, wo_ref,
    keep_ref, send_ref, mine_ref,
    x_ref, dy_ref, do_ref, dq_ref, dk_ref, dv_ref, ps, dss, grads,
    bias, gs, dx0, sums,
):
    core = lax.axis_index("core")
    chip = chip_index()
    wo = wo_ref.at[pl.ds(pl.multiple_of(core * HALF, HALF), HALF)]
    bias[...] = jnp.where(level_ref[...] > 0.5, 0.0, NEGATIVE)
    shift0 = mods_ref[0, 0:1, :]
    scale0 = 1.0 + mods_ref[1, 0:1, :]
    gate0 = mods_ref[2, 0:1, :]
    scale1 = 1.0 + mods_ref[1, 1:2, :]
    zero = jnp.zeros((1, D), F32)

    def norm_backward(dx, u, scale):
        factor, normed = norm_rows(u)
        shift_sum = jnp.sum(dx, axis=0, keepdims=True)
        scale_sum = jnp.sum(dx * normed, axis=0, keepdims=True)
        dn = dx * scale
        du = factor * (dn - normed * jnp.mean(dn * normed, axis=-1, keepdims=True))
        return du, shift_sum, scale_sum, jnp.sum(du, axis=0, keepdims=True)

    shift_sum, scale_sum, embed_sum, gate_sum = zero, zero, zero, zero
    for block in range(NBLK):
        rows = slice(block * BLK, (block + 1) * BLK)
        dx = dx_own_ref[rows, :].astype(F32) + dx_other_ref[rows, :].astype(F32)
        u = h1_ref[rows, :].astype(F32) + embeds_ref[1:2, :]
        du, a, b, c = norm_backward(dx, u, scale1)
        shift_sum, scale_sum, embed_sum = shift_sum + a, scale_sum + b, embed_sum + c
        g = g_ref[rows, :].astype(F32) + du
        gs[rows, :] = g
        gate_sum += jnp.sum(g * y0_ref[rows, :].astype(F32), axis=0, keepdims=True)
        dy = (g * gate0).astype(BF)
        dy_ref[rows, :] = dy
        do_ref[rows, :] = nt(dy, wo[...]).astype(BF)
        factor, normed = norm_rows(h_ref[rows, :].astype(F32) + embeds_ref[0:1, :])
        x_ref[rows, :] = (normed * scale0 + shift0).astype(BF)
    sums[2:3, :] = 0.5 * gate_sum
    sums[3:4, :] = 0.5 * shift_sum
    sums[4:5, :] = 0.5 * scale_sum
    sums[5:6, :] = gate1_ref[0:1, :]
    sums[7:8, :] = 0.5 * embed_sum
    attention_backward(
        q_ref, k_ref, v_ref, o_ref, do_ref, lse_ref, bias, dq_ref, dk_ref, dv_ref, ps, dss
    )
    shift_sum, scale_sum, embed_sum = zero, zero, zero
    for block in range(NBLK):
        rows = slice(block * BLK, (block + 1) * BLK)
        dx = unproject(rows, wq, wk, wv, dq_ref, dk_ref, dv_ref)
        dx0[rows, :] = dx
        u = h_ref[rows, :].astype(F32) + embeds_ref[0:1, :]
        du, a, b, c = norm_backward(dx, u, scale0)
        shift_sum, scale_sum, embed_sum = shift_sum + a, scale_sum + b, embed_sum + c
    sums[0:1, :] = shift_sum
    sums[1:2, :] = scale_sum
    sums[6:7, :] = embed_sum
    weight_grads(core, chip, x_ref, o_ref, dy_ref, dq_ref, dk_ref, dv_ref, grads)
    base = pl.multiple_of((chip % 4) * 32, 32)
    mine16 = pl.ds(pl.multiple_of(core * 16, 16), 16)
    other16 = pl.ds(pl.multiple_of((1 - core) * 16, 16), 16)
    chip_grads = grads.at[pl.ds(base, 32)]
    keep_ref[:, 0 : 5 * HALF] = (chip_grads[mine16, :] + grads1_ref[mine16, :]).astype(BF)
    send_ref[:, 0 : 5 * HALF] = (chip_grads[other16, :] + grads1_ref[other16, :]).astype(BF)
    total = jnp.concatenate([sums[:, 0:HALF], sums[:, HALF:D]], axis=0).astype(BF)
    keep_ref[:, 5 * HALF : 6 * HALF] = total
    send_ref[:, 5 * HALF : 6 * HALF] = total
    first_half = core == 0
    chip_rows = dx0.at[pl.ds(pl.multiple_of(chip * 2 * CAP, 8), 2 * CAP)]
    lower = chip_rows[0:16, :]
    upper = chip_rows[CAP - 4 : 2 * CAP, :]
    upper = jnp.concatenate([upper[4:16], upper[0:4]], axis=0)
    keep_ref[:, 6 * HALF : 8 * HALF] = jnp.where(first_half, lower, upper).astype(BF)
    send_ref[:, 6 * HALF : 8 * HALF] = jnp.where(first_half, upper, lower).astype(BF)
    g_rows = gs.at[pl.ds(pl.multiple_of(chip * 2 * CAP, 8), 2 * CAP)]
    mine_ref[...] = jnp.where(first_half, g_rows[0:CAP, :], g_rows[CAP : 2 * CAP, :])


def third(dx_own, dx_other, h1, h, g, level, y0, q, k, v, o, lse, grads1, gate1, embeds, mods, wq, wk, wv, wo):
    packed = sds((16, 8 * HALF), BF)
    half = pltpu.VMEM((SLOTS, HALF), BF)
    return call(
        third_kernel,
        (packed, packed, sds((CAP, D), F32)),
        [VSPEC] * 20,
        [
            pltpu.VMEM((SLOTS, D), BF), pltpu.VMEM((SLOTS, D), BF), half,
            half, half, half,
            pltpu.VMEM((2, SLOTS, SLOTS), BF), pltpu.VMEM((2, SLOTS, SLOTS), BF),
            pltpu.VMEM((DH, 5 * HALF), F32), pltpu.VMEM((SLOTS, 128), F32),
            pltpu.VMEM((SLOTS, D), F32), pltpu.VMEM((SLOTS, D), F32), pltpu.VMEM((8, D), F32),
        ],
        32,
    )(dx_own, dx_other, h1, h, g, level, y0, q, k, v, o, lse, grads1, gate1, embeds, mods, wq, wk, wv, wo)


def join_kernel(keep_ref, other_ref, out_ref):
    core = lax.axis_index("core")
    for part in range(3):
        cols = slice(part * HALF, (part + 1) * HALF)
        out_ref[:, pl.ds(pl.multiple_of(part * D + core * HALF, HALF), HALF)] = keep_ref[:, cols]
        out_ref[:, pl.ds(pl.multiple_of(part * D + (1 - core) * HALF, HALF), HALF)] = other_ref[:, cols]
    shared = slice(3 * HALF, 6 * HALF)
    both = keep_ref[:, shared].astype(F32) + other_ref[:, shared].astype(F32)
    out_ref[:, 3 * D :] = both.astype(BF)


def join(keep, other):
    return call(join_kernel, (sds((16, 9 * HALF), BF),), [VSPEC, VSPEC])(keep, other)[0]


def hidden_kernel(keep_ref, other_ref, mine_ref, rows_ref, picker_ref, cot_ref, embeds_ref, mods_ref, out_ref):
    cols = slice(6 * HALF, 8 * HALF)
    dx = keep_ref[:, cols].astype(F32) + other_ref[:, cols].astype(F32)
    dx = dx[0:CAP]
    factor, normed = norm_rows(rows_ref[...].astype(F32)[0:CAP] + embeds_ref[0:1, :])
    dn = dx * (1.0 + mods_ref[1, 0:1, :])
    du = factor * (dn - normed * jnp.mean(dn * normed, axis=-1, keepdims=True))
    rows = jnp.concatenate([mine_ref[...] + du, jnp.zeros((16 - CAP, D), F32)], axis=0).astype(BF)
    picker = picker_ref[...]
    placed = tn(picker, rows)
    taken = tn(picker, jnp.ones((16, 128), BF))
    taken = jnp.concatenate([taken] * 8, axis=1)
    out_ref[0] = jnp.where(taken > 0.5, placed.astype(BF), cot_ref[0])


def hidden_grad(keep, other, mine, rows, picker, cot, embeds, mods):
    specs = [VSPEC] * 5 + [LOAD] + [VSPEC] * 2
    return call(hidden_kernel, (sds((1, TOK, D), BF),), specs, pinned=False)(
        keep, other, mine, rows, picker, cot, embeds, mods
    )[0]


def swap_cores(x):
    return lax.ppermute(x, "core", [(0, 1), (1, 0)])


def chip_index():
    return (lax.axis_index("zl") * 4 + lax.axis_index("x")) * 4 + lax.axis_index("y")


def sequence_work(gathered, rows, picker, cot, embeds, mods, weights):
    wq, wk, wv, wo = weights
    mods = mods.transpose(1, 0, 2)
    other = swap_cores(gathered)
    q, k, v, o, lse, h, g, level, wq, wk, wv, wo = first(gathered, other, embeds, mods, wq, wk, wv, wo)
    o_other = swap_cores(o)
    dx, h1, y0, grads1, gate1 = second(o, o_other, h, g, level, embeds, mods, wq, wk, wv, wo)
    dx_other = swap_cores(dx)
    keep, send, mine = third(
        dx, dx_other, h1, h, g, level, y0, q, k, v, o, lse, grads1, gate1, embeds, mods, wq, wk, wv, wo
    )
    received = swap_cores(send)
    joined = join(keep, received)
    hidden = hidden_grad(keep, received, mine, rows, picker, cot, embeds, mods)
    return joined, hidden


def final_kernel(own_ref, one_ref, two_ref, three_ref, gq_ref, gk_ref, gv_ref, go_ref, embeds_ref, mods_ref):
    own, one, two, three = (r[...].astype(F32) for r in (own_ref, one_ref, two_ref, three_ref))
    total = (own + two) + (one + three)
    for part, ref in enumerate((gq_ref, gk_ref, gv_ref, go_ref)):
        ref[...] = total[:, part * D : (part + 1) * D]
    sums = jnp.concatenate([total[0:8, 4 * D :], total[8:16, 4 * D :]], axis=1)
    for kind in range(3):
        for section in range(2):
            row = 3 * section + kind
            mods_ref[kind, section : section + 1, :] = sums[row : row + 1]
    embeds_ref[...] = sums[6:8]


def dp_sum(joined):
    block = sds((16, D), F32)
    others = [lax.ppermute(joined, "dp", [(i, i ^ far) for i in range(4)]) for far in (1, 2, 3)]
    return call(
        final_kernel,
        (block, block, block, block, sds((2, D), F32), sds((3, 2, D), F32)),
        [VSPEC] * 4,
        pinned=False,
    )(joined, *others)


def shards(hidden, depth, cotangent, embeds, mods, w_query, w_key, w_value, w_out):
    payload, picker, rows = pick(depth, hidden, cotangent)
    spread = jnp.broadcast_to(payload[None], (CHIPS, PACKED, 128))
    gathered = lax.all_to_all(spread, ("zl", "x", "y"), 0, 0, tiled=True)
    joined, grad_hidden = sequence_work(
        gathered, rows, picker, cotangent, embeds, mods, (w_query, w_key, w_value, w_out)
    )
    gq, gk, gv, go, grad_embeds, grad_mods = dp_sum(joined)
    return (grad_hidden, gq, gk, gv, go, grad_embeds, grad_mods.transpose(1, 0, 2))


def solution(mesh):
    split = Mesh(mesh.devices.reshape(2, 4, 4, 2, 4), ("zl", "x", "y", "core", "dp"))
    ctx = ("zl", "x", "y", "core")
    in_specs = (P("dp", ctx, None), P("dp", ctx), P("dp", ctx, None)) + (P(),) * 6
    out_specs = (P("dp", ctx, None),) + (P(ctx, None),) * 4 + (P(), P())
    return jax.shard_map(shards, mesh=split, in_specs=in_specs, out_specs=out_specs, check_vma=False)
```

```python
import jax
import jax.numpy as jnp
from jax import lax
from jax.experimental import pallas as pl
from jax.experimental.pallas import tpu as pltpu
from jax.sharding import Mesh, PartitionSpec as P

D = 1024
H = 8
DH = 128
TOK = 128
CAP = 12
N_CTX = 64
CHIPS = 32
SLOTS = 768
HALF = 512
HEADS = 4
FORWARD_HEADS = 4
BACKWARD_HEADS = 4
TILES = 24
PACKED = (TILES + 1) * 8
BLK = 256
NBLK = SLOTS // BLK
EPSILON = 1e-06
NEGATIVE = -1e30
EMPTY = 64.0
SCALE = DH ** (-0.5)
SCALE2 = SCALE * 1.4426950408889634
BF = jnp.bfloat16
F32 = jnp.float32

VSPEC = pl.BlockSpec(memory_space=pltpu.VMEM)
LOAD = pl.BlockSpec(memory_space=pltpu.VMEM)
HSPEC = pl.BlockSpec(memory_space=pl.ANY)


def nn(a, b):
    return lax.dot_general(a, b, (((1,), (0,)), ((), ())), preferred_element_type=F32)


def nt(a, b):
    return lax.dot_general(a, b, (((1,), (1,)), ((), ())), preferred_element_type=F32)


def tn(a, b):
    return lax.dot_general(a, b, (((0,), (0,)), ((), ())), preferred_element_type=F32)


def sds(shape, dtype):
    return jax.ShapeDtypeStruct(shape, dtype)


def call(kernel, outs, in_specs, scratch=(), vmem=16, pinned=True):
    if pinned:
        outs = tuple(pltpu.VMEM(s.shape, s.dtype) for s in outs)
    run = pl.pallas_call(
        kernel,
        out_shape=outs,
        in_specs=in_specs,
        out_specs=tuple(VSPEC for _ in outs),
        scratch_shapes=list(scratch),
        compiler_params=pltpu.CompilerParams(vmem_limit_bytes=vmem * 1024 * 1024),
    )

    def placed(*args):
        spaces = [pltpu.VMEM if spec is VSPEC else pltpu.HBM for spec in in_specs]
        return run(*(pltpu.with_memory_space_constraint(a, m) for a, m in zip(args, spaces)))

    return placed


def pick_kernel(depth_ref, hidden_ref, cot_ref, payload_ref, picker_ref, rows_ref, both):
    depth = jnp.broadcast_to(depth_ref[...], (16, TOK))
    active = depth >= 2
    before = lax.broadcasted_iota(jnp.int32, (TOK, TOK), 0)
    upto = lax.broadcasted_iota(jnp.int32, (TOK, TOK), 1)
    upper = jnp.where(before <= upto, 1.0, 0.0).astype(BF)
    placing = nn(jnp.where(active, 1.0, 0.0).astype(BF), upper) - 1.0
    slot = lax.broadcasted_iota(jnp.int32, (16, TOK), 0)
    hit = active & (placing == slot.astype(F32)) & (slot < CAP)
    picker = jnp.where(hit, 1.0, 0.0)
    picker_ref[...] = picker.astype(BF)
    level = jnp.sum(picker * (depth - 1).astype(F32), axis=1, keepdims=True)
    rows = nn(picker.astype(BF), hidden_ref[0])
    both[0:CAP] = jnp.where(level > 0.5, rows, EMPTY)[0:CAP]
    both[CAP : 2 * CAP] = nn(picker.astype(BF), cot_ref[0])[0:CAP]
    lane = lax.broadcasted_iota(jnp.int32, (8, 128), 1)
    level = jnp.broadcast_to(level, (16, 128))
    tiles = [both[8 * r : 8 * r + 8, 128 * c : 128 * c + 128] for r in range(3) for c in range(8)]
    tiles.append(jnp.where(lane < 64, level[0:8], level[8:16]))
    payload_ref[...] = jnp.concatenate(tiles, axis=0).astype(BF)
    rows_ref[...] = both[0:16].astype(BF)


def pick(depth, hidden, cotangent):
    return call(
        pick_kernel,
        (sds((PACKED, 128), BF), sds((16, TOK), BF), sds((16, D), BF)),
        [LOAD, LOAD, LOAD],
        [pltpu.VMEM((2 * CAP, D), F32)],
    )(depth, hidden, cotangent)


def causal_bias():
    key = lax.broadcasted_iota(jnp.int32, (BLK, BLK), 0)
    query = lax.broadcasted_iota(jnp.int32, (BLK, BLK), 1)
    return jnp.where(key <= query, 0.0, NEGATIVE).astype(F32)


def norm_rows(u):
    factor = lax.rsqrt(jnp.mean(u * u, axis=-1, keepdims=True) + EPSILON)
    return factor, u * factor


def biased_scores(k, q, bias_ref, causal, upto):
    s = nt(k, q)
    bias = bias_ref[0:upto, :]
    s = s + jnp.concatenate([bias, bias], axis=1)
    last = s[upto - BLK : upto] + causal
    if upto == BLK:
        return last
    return jnp.concatenate([s[: upto - BLK], last], axis=0)


def row_blocks(body, carry=0):
    def step(block, carry):
        return body(pl.ds(pl.multiple_of(block * BLK, BLK), BLK), carry)

    return lax.fori_loop(0, NBLK, step, carry)


def head_cols(head):
    return pl.ds(pl.multiple_of(head * DH, DH), DH)


def attention_forward(q_ref, k_ref, v_ref, o_ref, lse_ref, bias_ref):
    causal = causal_bias()
    ones = jnp.ones((16, SLOTS), BF)

    def some_heads(step, carry):
        items = []
        for part in range(FORWARD_HEADS):
            head = step * FORWARD_HEADS + part
            cols = head_cols(head)
            vt = jnp.concatenate([v_ref[:, cols].T, ones], axis=0)
            items += [(head, cols, vt, block) for block in range(NBLK)]

        def start(head, cols, vt, block):
            upto = (block + 1) * BLK
            s = biased_scores(k_ref[0:upto, cols], q_ref[block * BLK : upto, cols], bias_ref, causal, upto)
            return s, jnp.max(s, axis=0, keepdims=True)

        def finish(head, cols, vt, block, s, top):
            upto = (block + 1) * BLK
            rows = slice(block * BLK, upto)
            e = jnp.exp2((s - top) * SCALE2).astype(BF)
            both = nn(vt[:, 0:upto], e)
            total = both[DH : DH + 1]
            o_ref[rows, cols] = (both[0:DH] * (1.0 / total)).T.astype(BF)
            lse_ref[pl.ds(head, 1), rows] = jnp.maximum(top * SCALE2 + jnp.log2(total), -1e25)

        state = start(*items[0])
        for i, item in enumerate(items):
            following = start(*items[i + 1]) if i + 1 < len(items) else None
            finish(*item, *state)
            state = following
        return carry

    lax.fori_loop(0, HEADS // FORWARD_HEADS, some_heads, 0)


def attention_backward(
    q_ref, k_ref, v_ref, o_ref, do_ref, lse_ref, bias_ref, dq_ref, dk_ref, dv_ref, ps, dss
):
    causal = causal_bias()

    def some_heads(step, carry):
        items = []
        for part in range(BACKWARD_HEADS):
            head = step * BACKWARD_HEADS + part
            cols = head_cols(head)
            kt = k_ref[:, cols].T
            items += [(head, part % 2, cols, kt, block) for block in range(NBLK)]

        def start(head, slot, cols, kt, block):
            upto = (block + 1) * BLK
            rows = slice(block * BLK, upto)
            s = biased_scores(k_ref[0:upto, cols], q_ref[rows, cols], bias_ref, causal, upto)
            return s, nt(v_ref[0:upto, cols], do_ref[rows, cols])

        def finish(head, slot, cols, kt, block, s, dp):
            upto = (block + 1) * BLK
            rows = slice(block * BLK, upto)
            product = do_ref[rows, cols].astype(F32) * o_ref[rows, cols].astype(F32)
            inner = jnp.sum(product.T, axis=0, keepdims=True)
            p = jnp.exp2(s * SCALE2 - lse_ref[pl.ds(head, 1), rows])
            ds = (p * (dp - inner)).astype(BF)
            ps[slot, 0:upto, rows] = p.astype(BF)
            dss[slot, 0:upto, rows] = ds
            dq_ref[rows, cols] = (nn(kt[:, 0:upto], ds).T * SCALE).astype(BF)

        def close(head, slot, cols):
            for block in range(NBLK):
                rows = slice(block * BLK, (block + 1) * BLK)
                later = slice(block * BLK, SLOTS)
                dv_ref[rows, cols] = nn(ps[slot, rows, later], do_ref[later, cols]).astype(BF)
                dk_ref[rows, cols] = (nn(dss[slot, rows, later], q_ref[later, cols]) * SCALE).astype(BF)

        state = start(*items[0])
        for i, item in enumerate(items):
            following = start(*items[i + 1]) if i + 1 < len(items) else None
            finish(*item, *state)
            state = following
            if item[-1] == NBLK - 1:
                close(*item[:3])
        return carry

    lax.fori_loop(0, HEADS // BACKWARD_HEADS, some_heads, 0)


def project(x, rows, wq, wk, wv, q_ref, k_ref, v_ref):
    q_ref[rows, :] = nn(x, wq[...]).astype(BF)
    k_ref[rows, :] = nn(x, wk[...]).astype(BF)
    v_ref[rows, :] = nn(x, wv[...]).astype(BF)


def unproject(rows, wq, wk, wv, dq_ref, dk_ref, dv_ref):
    return nt(dq_ref[rows, :], wq[...]) + nt(dk_ref[rows, :], wk[...]) + nt(dv_ref[rows, :], wv[...])


def place_block(block_ref, chip, base, start, hs, gs, level):
    tiles = block_ref[chip].astype(F32)
    rows_h = hs.at[pl.ds(base, 2 * CAP)]
    rows_g = gs.at[pl.ds(base, 2 * CAP)]
    rows_level = level.at[pl.ds(base, 2 * CAP)]
    for c in range(8):
        cols = slice(128 * c, 128 * c + 128)
        upper, middle, lower = (tiles[8 * (8 * r + c) : 8 * (8 * r + c) + 8] for r in range(3))
        rows_h[start : start + 8, cols] = upper
        rows_h[start + 8 : start + 12, cols] = middle[0:4]
        rows_g[start : start + 4, cols] = middle[4:8]
        rows_g[start + 4 : start + 12, cols] = lower
    depths = tiles[8 * TILES :]
    turned = pltpu.roll(depths, 64, 1)
    lane = lax.broadcasted_iota(jnp.int32, (8, 128), 1)
    rows_level[start : start + 8] = jnp.where(lane < 64, depths, turned)
    rows_level[start + 8 : start + 12] = jnp.where(lane < 64, turned, depths)[0:4]


def weight_grads(core, chip, x_ref, o_ref, dy_ref, dq_ref, dk_ref, dv_ref, grads):
    strip = pl.multiple_of((chip // 4) * DH, DH)
    xs = x_ref[:, pl.ds(strip, DH)]
    grads[:, 0:HALF] = tn(xs, dq_ref[...])
    grads[:, HALF : 2 * HALF] = tn(xs, dk_ref[...])
    grads[:, 2 * HALF : 3 * HALF] = tn(xs, dv_ref[...])
    own = jnp.where(chip // 16 == core, 1.0, 0.0).astype(F32)
    o_strip = pl.multiple_of(((chip // 4) % 4) * DH, DH)
    os = o_ref[:, pl.ds(o_strip, DH)]
    grads[:, 3 * HALF :] = tn(os, dy_ref[...]) * own


def first_kernel(
    own_ref, other_ref, embeds_ref, mods_ref, wq_hbm, wk_hbm, wv_hbm, wo_hbm,
    q_ref, k_ref, v_ref, o_ref, lse_ref, h_ref, g_ref, level_ref, x_ref, wq, wk, wv, wo,
    hs, gs, bias, sems,
):
    core = lax.axis_index("core")
    half = pl.ds(pl.multiple_of(core * HALF, HALF), HALF)
    copies = [
        pltpu.make_async_copy(source.at[:, half], target, sems.at[i])
        for i, (source, target) in enumerate(((wq_hbm, wq), (wk_hbm, wk), (wv_hbm, wv)))
    ]
    copies.append(pltpu.make_async_copy(wo_hbm, wo, sems.at[3]))
    for copy in copies:
        copy.start()

    def place(even_ref, odd_ref):
        def one_chip(chip, carry):
            base = pl.multiple_of(chip * 2 * CAP, 8)
            place_block(even_ref, chip, base, 0, hs, gs, level_ref)
            place_block(odd_ref, chip, base, CAP, hs, gs, level_ref)
            return carry

        lax.fori_loop(0, CHIPS, one_chip, 0)

    @pl.when(core == 0)
    def _():
        place(own_ref, other_ref)

    @pl.when(core == 1)
    def _():
        place(other_ref, own_ref)

    bias[...] = jnp.where(level_ref[...] > 0.5, 0.0, NEGATIVE)
    for copy in copies:
        copy.wait()
    embed = embeds_ref[0:1, :]
    shift = mods_ref[0, 0:1, :]
    scale = 1.0 + mods_ref[1, 0:1, :]

    def norm_block(rows):
        h = hs[rows, :]
        g_ref[rows, :] = gs[rows, :].astype(BF)
        h_ref[rows, :] = h.astype(BF)
        factor, normed = norm_rows(h + embed)
        x_ref[rows, :] = (normed * scale + shift).astype(BF)

    norm_block(pl.ds(0, BLK))
    for block in range(NBLK):
        if block + 1 < NBLK:
            norm_block(pl.ds((block + 1) * BLK, BLK))
        rows = pl.ds(block * BLK, BLK)
        project(x_ref[rows, :], rows, wq, wk, wv, q_ref, k_ref, v_ref)
    attention_forward(q_ref, k_ref, v_ref, o_ref, lse_ref, bias)


def first(own, other, embeds, mods, wq, wk, wv, wo):
    half = sds((SLOTS, HALF), BF)
    full = sds((SLOTS, D), BF)
    return call(
        first_kernel,
        (half, half, half, half, sds((8, SLOTS), F32), full, full, sds((SLOTS, 128), F32), full)
        + (sds((D, HALF), BF),) * 3
        + (sds((D, D), BF),),
        [VSPEC] * 4 + [HSPEC] * 4,
        [
            pltpu.VMEM((SLOTS, D), F32),
            pltpu.VMEM((SLOTS, D), F32),
            pltpu.VMEM((SLOTS, 128), F32),
            pltpu.SemaphoreType.DMA((4,)),
        ],
        16,
    )(own, other, embeds, mods, wq, wk, wv, wo)


def upstream_kernel(g_ref, level_ref, mods_ref, wo, dy_ref, do_ref):
    core = lax.axis_index("core")
    own_rows = pl.ds(pl.multiple_of(core * HALF, HALF), HALF)
    gate1 = mods_ref[2, 1:2, :]

    def some_rows(rows, carry):
        deep = jnp.where(level_ref[rows, 0:1] > 1.5, 1.0, 0.0)
        dy = (g_ref[rows, :].astype(F32) * deep * gate1).astype(BF)
        dy_ref[rows, :] = dy
        do_ref[rows, :] = nt(dy, wo[own_rows, :]).astype(BF)
        return carry

    row_blocks(some_rows)


def upstream_grads(g, level, mods, wo):
    return call(upstream_kernel, (sds((SLOTS, D), BF), sds((SLOTS, HALF), BF)), [VSPEC] * 4)(g, level, mods, wo)


def second_kernel(
    o_own_ref, o_other_ref, h_ref, level_ref, do_ref, embeds_ref, mods_ref, wq, wk, wv, wo,
    dx_ref, h1_ref, y0_ref, x_ref, o_ref, dq_ref, dk_ref, dv_ref,
    q_ref, k_ref, v_ref, lse_ref, ps, dss, bias,
):
    core = lax.axis_index("core")
    bias[...] = jnp.where(level_ref[...] > 1.5, 0.0, NEGATIVE)
    own_rows = pl.ds(pl.multiple_of(core * HALF, HALF), HALF)
    other_rows = pl.ds(pl.multiple_of((1 - core) * HALF, HALF), HALF)
    gate0 = mods_ref[2, 0:1, :]
    embed = embeds_ref[1:2, :]
    shift = mods_ref[0, 1:2, :]
    scale = 1.0 + mods_ref[1, 1:2, :]

    def forward_rows(rows):
        y0 = nn(o_own_ref[rows, :], wo[own_rows, :]) + nn(o_other_ref[rows, :], wo[other_rows, :])
        y0_ref[rows, :] = y0.astype(BF)
        h1 = (h_ref[rows, :].astype(F32) + gate0 * y0).astype(BF)
        h1_ref[rows, :] = h1
        factor, normed = norm_rows(h1.astype(F32) + embed)
        x_ref[rows, :] = (normed * scale + shift).astype(BF)

    forward_rows(pl.ds(0, BLK))
    for block in range(NBLK):
        if block + 1 < NBLK:
            forward_rows(pl.ds((block + 1) * BLK, BLK))
        rows = pl.ds(block * BLK, BLK)
        project(x_ref[rows, :], rows, wq, wk, wv, q_ref, k_ref, v_ref)
    attention_forward(q_ref, k_ref, v_ref, o_ref, lse_ref, bias)
    attention_backward(
        q_ref, k_ref, v_ref, o_ref, do_ref, lse_ref, bias, dq_ref, dk_ref, dv_ref, ps, dss
    )

    def backward_rows(rows, carry):
        dx_ref[rows, :] = unproject(rows, wq, wk, wv, dq_ref, dk_ref, dv_ref).astype(BF)
        return carry

    row_blocks(backward_rows)


def second(o_own, o_other, h, level, do, embeds, mods, wq, wk, wv, wo):
    full = sds((SLOTS, D), BF)
    half = sds((SLOTS, HALF), BF)
    scratch = pltpu.VMEM((SLOTS, HALF), BF)
    return call(
        second_kernel,
        (full, full, full, full, half, half, half, half),
        [VSPEC] * 11,
        [
            scratch, scratch, scratch, pltpu.VMEM((8, SLOTS), F32),
            pltpu.VMEM((2, SLOTS, SLOTS), BF), pltpu.VMEM((2, SLOTS, SLOTS), BF),
            pltpu.VMEM((SLOTS, 128), F32),
        ],
        20,
    )(o_own, o_other, h, level, do, embeds, mods, wq, wk, wv, wo)


def sums_kernel(x_ref, o_ref, dy_ref, dq_ref, dk_ref, dv_ref, g_ref, level_ref, wo, grads_ref, gate_ref, grads):
    core = lax.axis_index("core")
    chip = chip_index()
    own_rows = pl.ds(pl.multiple_of(core * HALF, HALF), HALF)

    def some_rows(rows, gate_sum):
        y1 = nn(o_ref[rows, :], wo[own_rows, :])
        deep = jnp.where(level_ref[rows, 0:1] > 1.5, 1.0, 0.0)
        return gate_sum + jnp.sum(g_ref[rows, :].astype(F32) * deep * y1, axis=0, keepdims=True)

    gate_sum = row_blocks(some_rows, jnp.zeros((1, D), F32))
    gate_ref[...] = jnp.broadcast_to(gate_sum, (8, D))
    weight_grads(core, chip, x_ref, o_ref, dy_ref, dq_ref, dk_ref, dv_ref, grads)
    grads_ref[...] = grads[pl.ds(pl.multiple_of((chip % 4) * 32, 32), 32), :]


def second_sums(x, o, dy, dq, dk, dv, g, level, wo):
    return call(
        sums_kernel,
        (sds((32, 5 * HALF), F32), sds((8, D), F32)),
        [VSPEC] * 9,
        [pltpu.VMEM((DH, 5 * HALF), F32)],
    )(x, o, dy, dq, dk, dv, g, level, wo)


def third_kernel(
    dx_own_ref, dx_other_ref, h1_ref, h_ref, x_ref, g_ref, level_ref, y0_ref,
    q_ref, k_ref, v_ref, o_ref, lse_ref, grads1_ref, gate1_ref, embeds_ref, mods_ref,
    wq, wk, wv, wo_ref,
    keep_ref, send_ref, mine_ref,
    dy_ref, do_ref, dq_ref, dk_ref, dv_ref, ps, dss, grads,
    bias, gs, dx0, sums,
):
    core = lax.axis_index("core")
    chip = chip_index()
    wo = wo_ref.at[pl.ds(pl.multiple_of(core * HALF, HALF), HALF)]
    bias[...] = jnp.where(level_ref[...] > 0.5, 0.0, NEGATIVE)
    scale0 = 1.0 + mods_ref[1, 0:1, :]
    gate0 = mods_ref[2, 0:1, :]
    scale1 = 1.0 + mods_ref[1, 1:2, :]
    zero = jnp.zeros((1, D), F32)

    def norm_backward(dx, u, scale):
        factor, normed = norm_rows(u)
        shift_sum = jnp.sum(dx, axis=0, keepdims=True)
        scale_sum = jnp.sum(dx * normed, axis=0, keepdims=True)
        dn = dx * scale
        du = factor * (dn - normed * jnp.mean(dn * normed, axis=-1, keepdims=True))
        return du, shift_sum, scale_sum, jnp.sum(du, axis=0, keepdims=True)

    def later_rows(rows, carry):
        shift_sum, scale_sum, embed_sum, gate_sum = carry
        dx = dx_own_ref[rows, :].astype(F32) + dx_other_ref[rows, :].astype(F32)
        u = h1_ref[rows, :].astype(F32) + embeds_ref[1:2, :]
        du, a, b, c = norm_backward(dx, u, scale1)
        shift_sum, scale_sum, embed_sum = shift_sum + a, scale_sum + b, embed_sum + c
        g = g_ref[rows, :].astype(F32) + du
        gs[rows, :] = g
        gate_sum += jnp.sum(g * y0_ref[rows, :].astype(F32), axis=0, keepdims=True)
        dy = (g * gate0).astype(BF)
        dy_ref[rows, :] = dy
        do_ref[rows, :] = nt(dy, wo[...]).astype(BF)
        return shift_sum, scale_sum, embed_sum, gate_sum

    shift_sum, scale_sum, embed_sum, gate_sum = row_blocks(later_rows, (zero,) * 4)
    sums[2:3, :] = 0.5 * gate_sum
    sums[3:4, :] = 0.5 * shift_sum
    sums[4:5, :] = 0.5 * scale_sum
    sums[5:6, :] = gate1_ref[0:1, :]
    sums[7:8, :] = 0.5 * embed_sum
    attention_backward(
        q_ref, k_ref, v_ref, o_ref, do_ref, lse_ref, bias, dq_ref, dk_ref, dv_ref, ps, dss
    )

    def earlier_rows(rows, carry):
        shift_sum, scale_sum, embed_sum = carry
        dx = unproject(rows, wq, wk, wv, dq_ref, dk_ref, dv_ref)
        dx0[rows, :] = dx
        u = h_ref[rows, :].astype(F32) + embeds_ref[0:1, :]
        du, a, b, c = norm_backward(dx, u, scale0)
        shift_sum, scale_sum, embed_sum = shift_sum + a, scale_sum + b, embed_sum + c
        return shift_sum, scale_sum, embed_sum

    shift_sum, scale_sum, embed_sum = row_blocks(earlier_rows, (zero,) * 3)
    sums[0:1, :] = shift_sum
    sums[1:2, :] = scale_sum
    sums[6:7, :] = embed_sum
    weight_grads(core, chip, x_ref, o_ref, dy_ref, dq_ref, dk_ref, dv_ref, grads)
    base = pl.multiple_of((chip % 4) * 32, 32)
    mine16 = pl.ds(pl.multiple_of(core * 16, 16), 16)
    other16 = pl.ds(pl.multiple_of((1 - core) * 16, 16), 16)
    chip_grads = grads.at[pl.ds(base, 32)]
    keep_ref[:, 0 : 5 * HALF] = (chip_grads[mine16, :] + grads1_ref[mine16, :]).astype(BF)
    send_ref[:, 0 : 5 * HALF] = (chip_grads[other16, :] + grads1_ref[other16, :]).astype(BF)
    total = jnp.concatenate([sums[:, 0:HALF], sums[:, HALF:D]], axis=0).astype(BF)
    keep_ref[:, 5 * HALF : 6 * HALF] = total
    send_ref[:, 5 * HALF : 6 * HALF] = total
    first_half = core == 0
    chip_rows = dx0.at[pl.ds(pl.multiple_of(chip * 2 * CAP, 8), 2 * CAP)]
    lower = chip_rows[0:16, :]
    upper = chip_rows[CAP - 4 : 2 * CAP, :]
    upper = jnp.concatenate([upper[4:16], upper[0:4]], axis=0)
    keep_ref[:, 6 * HALF : 8 * HALF] = jnp.where(first_half, lower, upper).astype(BF)
    send_ref[:, 6 * HALF : 8 * HALF] = jnp.where(first_half, upper, lower).astype(BF)
    g_rows = gs.at[pl.ds(pl.multiple_of(chip * 2 * CAP, 8), 2 * CAP)]
    mine_ref[...] = jnp.where(first_half, g_rows[0:CAP, :], g_rows[CAP : 2 * CAP, :])


def third(dx_own, dx_other, h1, h, x, g, level, y0, q, k, v, o, lse, grads1, gate1, embeds, mods, wq, wk, wv, wo):
    packed = sds((16, 8 * HALF), BF)
    half = pltpu.VMEM((SLOTS, HALF), BF)
    return call(
        third_kernel,
        (packed, packed, sds((CAP, D), F32)),
        [VSPEC] * 21,
        [
            pltpu.VMEM((SLOTS, D), BF), half, half, half, half,
            pltpu.VMEM((2, SLOTS, SLOTS), BF), pltpu.VMEM((2, SLOTS, SLOTS), BF),
            pltpu.VMEM((DH, 5 * HALF), F32), pltpu.VMEM((SLOTS, 128), F32),
            pltpu.VMEM((SLOTS, D), F32), pltpu.VMEM((SLOTS, D), F32), pltpu.VMEM((8, D), F32),
        ],
        28,
    )(dx_own, dx_other, h1, h, x, g, level, y0, q, k, v, o, lse, grads1, gate1, embeds, mods, wq, wk, wv, wo)


def join_kernel(keep_ref, other_ref, left_ref, right_ref):
    core = lax.axis_index("core")
    for part, (out, start) in enumerate(((left_ref, 0), (left_ref, D), (right_ref, 0))):
        cols = slice(part * HALF, (part + 1) * HALF)
        out[:, pl.ds(pl.multiple_of(start + core * HALF, HALF), HALF)] = keep_ref[:, cols]
        out[:, pl.ds(pl.multiple_of(start + (1 - core) * HALF, HALF), HALF)] = other_ref[:, cols]
    shared = slice(3 * HALF, 6 * HALF)
    both = (keep_ref[:, shared].astype(F32) + other_ref[:, shared].astype(F32)).astype(BF)
    right_ref[:, D : 2 * D] = both[:, 0:D]
    left_ref[:, 2 * D :] = both[:, D : D + 256]
    right_ref[:, 2 * D :] = both[:, D + 256 :]


def join(keep, other):
    half = sds((16, 2 * D + 256), BF)
    return call(join_kernel, (half, half), [VSPEC, VSPEC])(keep, other)


def hidden_kernel(keep_ref, other_ref, mine_ref, rows_ref, picker_ref, cot_ref, embeds_ref, mods_ref, out_ref):
    cols = slice(6 * HALF, 8 * HALF)
    dx = keep_ref[:, cols].astype(F32) + other_ref[:, cols].astype(F32)
    dx = dx[0:CAP]
    factor, normed = norm_rows(rows_ref[...].astype(F32)[0:CAP] + embeds_ref[0:1, :])
    dn = dx * (1.0 + mods_ref[1, 0:1, :])
    du = factor * (dn - normed * jnp.mean(dn * normed, axis=-1, keepdims=True))
    rows = jnp.concatenate([mine_ref[...] + du, jnp.zeros((16 - CAP, D), F32)], axis=0).astype(BF)
    picker = picker_ref[...]
    placed = tn(picker, rows)
    taken = tn(picker, jnp.ones((16, 128), BF))
    taken = jnp.concatenate([taken] * 8, axis=1)
    out_ref[0] = jnp.where(taken > 0.5, placed.astype(BF), cot_ref[0])


def hidden_grad(keep, other, mine, rows, picker, cot, embeds, mods):
    specs = [VSPEC] * 5 + [LOAD] + [VSPEC] * 2
    return call(hidden_kernel, (sds((1, TOK, D), BF),), specs, pinned=False)(
        keep, other, mine, rows, picker, cot, embeds, mods
    )[0]


def swap_cores(x):
    return lax.ppermute(x, "core", [(0, 1), (1, 0)])


def chip_index():
    return (lax.axis_index("zl") * 4 + lax.axis_index("x")) * 4 + lax.axis_index("y")


def sequence_work(gathered, rows, picker, cot, embeds, mods, weights):
    wq, wk, wv, wo = weights
    mods = mods.transpose(1, 0, 2)
    other = swap_cores(gathered)
    q, k, v, o, lse, h, g, level, x, wq, wk, wv, wo = first(gathered, other, embeds, mods, wq, wk, wv, wo)
    o_other = swap_cores(o)
    dy1, do1 = upstream_grads(g, level, mods, wo)
    dx, h1, y0, x1, o1, dq1, dk1, dv1 = second(o, o_other, h, level, do1, embeds, mods, wq, wk, wv, wo)
    dx_other = swap_cores(dx)
    grads1, gate1 = second_sums(x1, o1, dy1, dq1, dk1, dv1, g, level, wo)
    keep, send, mine = third(
        dx, dx_other, h1, h, x, g, level, y0, q, k, v, o, lse, grads1, gate1, embeds, mods, wq, wk, wv, wo
    )
    received = swap_cores(send)
    joined = join(keep, received)
    hidden = hidden_grad(keep, received, mine, rows, picker, cot, embeds, mods)
    return joined, hidden


def pair_kernel(left_ref, left_other_ref, right_ref, right_other_ref, left_out, right_out):
    left_out[...] = (left_ref[...].astype(F32) + left_other_ref[...].astype(F32)).astype(BF)
    right_out[...] = (right_ref[...].astype(F32) + right_other_ref[...].astype(F32)).astype(BF)


def final_kernel(left_ref, left_other_ref, right_ref, right_other_ref, gq_ref, gk_ref, gv_ref, go_ref, embeds_ref, mods_ref):
    left = left_ref[...].astype(F32) + left_other_ref[...].astype(F32)
    right = right_ref[...].astype(F32) + right_other_ref[...].astype(F32)
    gq_ref[...] = left[:, 0:D]
    gk_ref[...] = left[:, D : 2 * D]
    gv_ref[...] = right[:, 0:D]
    go_ref[...] = right[:, D : 2 * D]
    rest = jnp.concatenate([left[:, 2 * D :], right[:, 2 * D :]], axis=1)
    sums = jnp.concatenate([rest[0:8], rest[8:16]], axis=1)
    for kind in range(3):
        for section in range(2):
            row = 3 * section + kind
            mods_ref[kind, section : section + 1, :] = sums[row : row + 1]
    embeds_ref[...] = sums[6:8]


def dp_sum(left, right):
    def swap(x, far):
        return lax.ppermute(x, "dp", [(i, i ^ far) for i in range(4)])

    half = sds(left.shape, BF)
    left, right = call(pair_kernel, (half, half), [VSPEC] * 4)(left, swap(left, 1), right, swap(right, 3))
    block = sds((16, D), F32)
    return call(
        final_kernel,
        (block, block, block, block, sds((2, D), F32), sds((3, 2, D), F32)),
        [VSPEC] * 4,
        pinned=False,
    )(left, swap(left, 3), right, swap(right, 1))


def shards(hidden, depth, cotangent, embeds, mods, w_query, w_key, w_value, w_out):
    payload, picker, rows = pick(depth, hidden, cotangent)
    spread = jnp.broadcast_to(payload[None], (CHIPS, PACKED, 128))
    gathered = lax.all_to_all(spread, ("zl", "x", "y"), 0, 0, tiled=True)
    joined, grad_hidden = sequence_work(
        gathered, rows, picker, cotangent, embeds, mods, (w_query, w_key, w_value, w_out)
    )
    gq, gk, gv, go, grad_embeds, grad_mods = dp_sum(*joined)
    return (grad_hidden, gq, gk, gv, go, grad_embeds, grad_mods.transpose(1, 0, 2))


def solution(mesh):
    split = Mesh(mesh.devices.reshape(2, 4, 4, 2, 4), ("zl", "x", "y", "core", "dp"))
    ctx = ("zl", "x", "y", "core")
    in_specs = (P("dp", ctx, None), P("dp", ctx), P("dp", ctx, None)) + (P(),) * 6
    out_specs = (P("dp", ctx, None),) + (P(ctx, None),) * 4 + (P(), P())
    return jax.shard_map(shards, mesh=split, in_specs=in_specs, out_specs=out_specs, check_vma=False)
```

```python
import jax
import jax.numpy as jnp
from jax import lax
from jax.experimental import pallas as pl
from jax.experimental.pallas import tpu as pltpu
from jax.sharding import Mesh, PartitionSpec as P

D = 1024
H = 8
DH = 128
TOK = 128
CAP = 12
N_CTX = 64
CHIPS = 32
SLOTS = 768
HALF = 512
HEADS = 4
FORWARD_HEADS = 4
BACKWARD_HEADS = 4
TILES = 24
PACKED = (TILES + 1) * 8
BLK = 256
NBLK = SLOTS // BLK
EPSILON = 1e-06
NEGATIVE = -1e30
EMPTY = 64.0
SCALE = DH ** (-0.5)
SCALE2 = SCALE * 1.4426950408889634
BF = jnp.bfloat16
F32 = jnp.float32

VSPEC = pl.BlockSpec(memory_space=pltpu.VMEM)
LOAD = pl.BlockSpec(memory_space=pltpu.VMEM)
HSPEC = pl.BlockSpec(memory_space=pl.ANY)


def nn(a, b):
    return lax.dot_general(a, b, (((1,), (0,)), ((), ())), preferred_element_type=F32)


def nt(a, b):
    return lax.dot_general(a, b, (((1,), (1,)), ((), ())), preferred_element_type=F32)


def tn(a, b):
    return lax.dot_general(a, b, (((0,), (0,)), ((), ())), preferred_element_type=F32)


def sds(shape, dtype):
    return jax.ShapeDtypeStruct(shape, dtype)


def call(kernel, outs, in_specs, scratch=(), vmem=16, pinned=True):
    if pinned:
        outs = tuple(pltpu.VMEM(s.shape, s.dtype) for s in outs)
    run = pl.pallas_call(
        kernel,
        out_shape=outs,
        in_specs=in_specs,
        out_specs=tuple(VSPEC for _ in outs),
        scratch_shapes=list(scratch),
        compiler_params=pltpu.CompilerParams(vmem_limit_bytes=vmem * 1024 * 1024),
    )

    def placed(*args):
        spaces = [pltpu.VMEM if spec is VSPEC else pltpu.HBM for spec in in_specs]
        return run(*(pltpu.with_memory_space_constraint(a, m) for a, m in zip(args, spaces)))

    return placed


def pick_kernel(depth_ref, hidden_ref, cot_ref, payload_ref, picker_ref, rows_ref, both):
    depth = jnp.broadcast_to(depth_ref[...], (16, TOK))
    active = depth >= 2
    before = lax.broadcasted_iota(jnp.int32, (TOK, TOK), 0)
    upto = lax.broadcasted_iota(jnp.int32, (TOK, TOK), 1)
    upper = jnp.where(before <= upto, 1.0, 0.0).astype(BF)
    placing = nn(jnp.where(active, 1.0, 0.0).astype(BF), upper) - 1.0
    slot = lax.broadcasted_iota(jnp.int32, (16, TOK), 0)
    hit = active & (placing == slot.astype(F32)) & (slot < CAP)
    picker = jnp.where(hit, 1.0, 0.0)
    picker_ref[...] = picker.astype(BF)
    level = jnp.sum(picker * (depth - 1).astype(F32), axis=1, keepdims=True)
    rows = nn(picker.astype(BF), hidden_ref[0])
    both[0:CAP] = jnp.where(level > 0.5, rows, EMPTY)[0:CAP]
    both[CAP : 2 * CAP] = nn(picker.astype(BF), cot_ref[0])[0:CAP]
    lane = lax.broadcasted_iota(jnp.int32, (8, 128), 1)
    level = jnp.broadcast_to(level, (16, 128))
    tiles = [both[8 * r : 8 * r + 8, 128 * c : 128 * c + 128] for r in range(3) for c in range(8)]
    tiles.append(jnp.where(lane < 64, level[0:8], level[8:16]))
    payload_ref[...] = jnp.concatenate(tiles, axis=0).astype(BF)
    rows_ref[...] = both[0:16].astype(BF)


def pick(depth, hidden, cotangent):
    return call(
        pick_kernel,
        (sds((PACKED, 128), BF), sds((16, TOK), BF), sds((16, D), BF)),
        [LOAD, LOAD, LOAD],
        [pltpu.VMEM((2 * CAP, D), F32)],
    )(depth, hidden, cotangent)


def causal_bias():
    key = lax.broadcasted_iota(jnp.int32, (BLK, BLK), 0)
    query = lax.broadcasted_iota(jnp.int32, (BLK, BLK), 1)
    return jnp.where(key <= query, 0.0, NEGATIVE).astype(F32)


def fill_bias(level_ref, least):
    lane = lax.broadcasted_iota(jnp.int32, (SLOTS, DH), 1)
    return jnp.where((level_ref[...] > least) | (lane > 0), 0.0, NEGATIVE).astype(BF)


def norm_rows(u):
    factor = lax.rsqrt(jnp.mean(u * u, axis=-1, keepdims=True) + EPSILON)
    return factor, u * factor


def biased_scores(k, q, bias_ref, causal, upto):
    lane = lax.broadcasted_iota(jnp.int32, (BLK, DH), 1)
    unit = jnp.where(lane == 0, 1.0, 0.0).astype(BF)
    s = nt(jnp.concatenate([k, bias_ref[0:upto, :]], axis=1), jnp.concatenate([q, unit], axis=1))
    last = s[upto - BLK : upto] + causal
    if upto == BLK:
        return last
    return jnp.concatenate([s[: upto - BLK], last], axis=0)


def row_blocks(body, carry=0):
    def step(block, carry):
        return body(pl.ds(pl.multiple_of(block * BLK, BLK), BLK), carry)

    return lax.fori_loop(0, NBLK, step, carry)


def head_cols(head):
    return pl.ds(pl.multiple_of(head * DH, DH), DH)


def attention_forward(q_ref, k_ref, v_ref, o_ref, lse_ref, bias_ref):
    causal = causal_bias()
    ones = jnp.ones((16, SLOTS), BF)

    def some_heads(step, carry):
        items = []
        for part in range(FORWARD_HEADS):
            head = step * FORWARD_HEADS + part
            cols = head_cols(head)
            vt = jnp.concatenate([v_ref[:, cols].T, ones], axis=0)
            items += [(head, cols, vt, block) for block in range(NBLK)]

        def start(head, cols, vt, block):
            upto = (block + 1) * BLK
            s = biased_scores(k_ref[0:upto, cols], q_ref[block * BLK : upto, cols], bias_ref, causal, upto)
            return s, jnp.max(s, axis=0, keepdims=True)

        def finish(head, cols, vt, block, s, top):
            upto = (block + 1) * BLK
            rows = slice(block * BLK, upto)
            e = jnp.exp2((s - top) * SCALE2).astype(BF)
            both = nn(vt[:, 0:upto], e)
            total = both[DH : DH + 1]
            o_ref[rows, cols] = (both[0:DH] * (1.0 / total)).T.astype(BF)
            lse_ref[pl.ds(head, 1), rows] = jnp.maximum(top * SCALE2 + jnp.log2(total), -1e25)

        states = [start(*item) for item in items[:2]]
        for i, item in enumerate(items):
            if i + 2 < len(items):
                states.append(start(*items[i + 2]))
            finish(*item, *states[i])
        return carry

    lax.fori_loop(0, HEADS // FORWARD_HEADS, some_heads, 0)


def attention_backward(
    q_ref, k_ref, v_ref, o_ref, do_ref, lse_ref, bias_ref, dq_ref, dk_ref, dv_ref, ps, dss
):
    causal = causal_bias()

    def some_heads(step, carry):
        items = []
        for part in range(BACKWARD_HEADS):
            head = step * BACKWARD_HEADS + part
            cols = head_cols(head)
            kt = k_ref[:, cols].T
            items += [(head, part % 2, cols, kt, block) for block in range(NBLK)]

        def start(head, slot, cols, kt, block):
            upto = (block + 1) * BLK
            rows = slice(block * BLK, upto)
            s = biased_scores(k_ref[0:upto, cols], q_ref[rows, cols], bias_ref, causal, upto)
            return s, nt(v_ref[0:upto, cols], do_ref[rows, cols])

        def finish(head, slot, cols, kt, block, s, dp):
            upto = (block + 1) * BLK
            rows = slice(block * BLK, upto)
            product = do_ref[rows, cols].astype(F32) * o_ref[rows, cols].astype(F32)
            inner = jnp.sum(product.T, axis=0, keepdims=True)
            p = jnp.exp2(s * SCALE2 - lse_ref[pl.ds(head, 1), rows])
            ds = (p * (dp - inner)).astype(BF)
            ps[slot, 0:upto, rows] = p.astype(BF)
            dss[slot, 0:upto, rows] = ds
            dq_ref[rows, cols] = (nn(kt[:, 0:upto], ds).T * SCALE).astype(BF)

        def close(head, slot, cols):
            for block in range(NBLK):
                rows = slice(block * BLK, (block + 1) * BLK)
                later = slice(block * BLK, SLOTS)
                dv_ref[rows, cols] = nn(ps[slot, rows, later], do_ref[later, cols]).astype(BF)
                dk_ref[rows, cols] = (nn(dss[slot, rows, later], q_ref[later, cols]) * SCALE).astype(BF)

        states = [start(*item) for item in items[:1]]
        for i, item in enumerate(items):
            if i + 1 < len(items):
                states.append(start(*items[i + 1]))
            finish(*item, *states[i])
            if item[-1] == NBLK - 1:
                close(*item[:3])
        return carry

    lax.fori_loop(0, HEADS // BACKWARD_HEADS, some_heads, 0)


def project(x, rows, wq, wk, wv, q_ref, k_ref, v_ref):
    q_ref[rows, :] = nn(x, wq[...]).astype(BF)
    k_ref[rows, :] = nn(x, wk[...]).astype(BF)
    v_ref[rows, :] = nn(x, wv[...]).astype(BF)


def unproject(rows, wq, wk, wv, dq_ref, dk_ref, dv_ref):
    return nt(dq_ref[rows, :], wq[...]) + nt(dk_ref[rows, :], wk[...]) + nt(dv_ref[rows, :], wv[...])


def place_block(block_ref, chip, base, start, hs, gs, level):
    tiles = block_ref[chip].astype(F32)
    rows_h = hs.at[pl.ds(base, 2 * CAP)]
    rows_g = gs.at[pl.ds(base, 2 * CAP)]
    rows_level = level.at[pl.ds(base, 2 * CAP)]
    for c in range(8):
        cols = slice(128 * c, 128 * c + 128)
        upper, middle, lower = (tiles[8 * (8 * r + c) : 8 * (8 * r + c) + 8] for r in range(3))
        rows_h[start : start + 8, cols] = upper
        rows_h[start + 8 : start + 12, cols] = middle[0:4]
        rows_g[start : start + 4, cols] = middle[4:8]
        rows_g[start + 4 : start + 12, cols] = lower
    depths = tiles[8 * TILES :]
    turned = pltpu.roll(depths, 64, 1)
    lane = lax.broadcasted_iota(jnp.int32, (8, 128), 1)
    rows_level[start : start + 8] = jnp.where(lane < 64, depths, turned)
    rows_level[start + 8 : start + 12] = jnp.where(lane < 64, turned, depths)[0:4]


def weight_grads(core, chip, x_ref, o_ref, dy_ref, dq_ref, dk_ref, dv_ref, grads):
    strip = pl.multiple_of((chip // 4) * DH, DH)
    xs = x_ref[:, pl.ds(strip, DH)]
    grads[:, 0:HALF] = tn(xs, dq_ref[...])
    grads[:, HALF : 2 * HALF] = tn(xs, dk_ref[...])
    grads[:, 2 * HALF : 3 * HALF] = tn(xs, dv_ref[...])
    own = jnp.where(chip // 16 == core, 1.0, 0.0).astype(F32)
    o_strip = pl.multiple_of(((chip // 4) % 4) * DH, DH)
    os = o_ref[:, pl.ds(o_strip, DH)]
    grads[:, 3 * HALF :] = tn(os, dy_ref[...]) * own


def first_kernel(
    own_ref, other_ref, embeds_ref, mods_ref, wq_hbm, wk_hbm, wv_hbm, wo_hbm,
    q_ref, k_ref, v_ref, o_ref, lse_ref, h_ref, g_ref, level_ref, x_ref, wq, wk, wv, wo,
    hs, gs, bias, sems,
):
    core = lax.axis_index("core")
    half = pl.ds(pl.multiple_of(core * HALF, HALF), HALF)
    copies = [
        pltpu.make_async_copy(source.at[:, half], target, sems.at[i])
        for i, (source, target) in enumerate(((wq_hbm, wq), (wk_hbm, wk), (wv_hbm, wv)))
    ]
    copies.append(pltpu.make_async_copy(wo_hbm, wo, sems.at[3]))
    for copy in copies:
        copy.start()

    def place(even_ref, odd_ref):
        def one_chip(chip, carry):
            base = pl.multiple_of(chip * 2 * CAP, 8)
            place_block(even_ref, chip, base, 0, hs, gs, level_ref)
            place_block(odd_ref, chip, base, CAP, hs, gs, level_ref)
            return carry

        lax.fori_loop(0, CHIPS, one_chip, 0, unroll=4)

    @pl.when(core == 0)
    def _():
        place(own_ref, other_ref)

    @pl.when(core == 1)
    def _():
        place(other_ref, own_ref)

    bias[...] = fill_bias(level_ref, 0.5)
    for copy in copies:
        copy.wait()
    embed = embeds_ref[0:1, :]
    shift = mods_ref[0, 0:1, :]
    scale = 1.0 + mods_ref[1, 0:1, :]

    def norm_block(rows):
        h = hs[rows, :]
        g_ref[rows, :] = gs[rows, :].astype(BF)
        h_ref[rows, :] = h.astype(BF)
        factor, normed = norm_rows(h + embed)
        x_ref[rows, :] = (normed * scale + shift).astype(BF)

    norm_block(pl.ds(0, BLK))
    for block in range(NBLK):
        if block + 1 < NBLK:
            norm_block(pl.ds((block + 1) * BLK, BLK))
        rows = pl.ds(block * BLK, BLK)
        project(x_ref[rows, :], rows, wq, wk, wv, q_ref, k_ref, v_ref)
    attention_forward(q_ref, k_ref, v_ref, o_ref, lse_ref, bias)


def first(own, other, embeds, mods, wq, wk, wv, wo):
    half = sds((SLOTS, HALF), BF)
    full = sds((SLOTS, D), BF)
    return call(
        first_kernel,
        (half, half, half, half, sds((8, SLOTS), F32), full, full, sds((SLOTS, 128), F32), full)
        + (sds((D, HALF), BF),) * 3
        + (sds((D, D), BF),),
        [VSPEC] * 4 + [HSPEC] * 4,
        [
            pltpu.VMEM((SLOTS, D), F32),
            pltpu.VMEM((SLOTS, D), F32),
            pltpu.VMEM((SLOTS, 128), BF),
            pltpu.SemaphoreType.DMA((4,)),
        ],
        16,
    )(own, other, embeds, mods, wq, wk, wv, wo)


def upstream_kernel(g_ref, level_ref, mods_ref, wo, dy_ref, do_ref):
    core = lax.axis_index("core")
    own_rows = pl.ds(pl.multiple_of(core * HALF, HALF), HALF)
    gate1 = mods_ref[2, 1:2, :]

    def some_rows(rows, carry):
        deep = jnp.where(level_ref[rows, 0:1] > 1.5, 1.0, 0.0)
        dy = (g_ref[rows, :].astype(F32) * deep * gate1).astype(BF)
        dy_ref[rows, :] = dy
        do_ref[rows, :] = nt(dy, wo[own_rows, :]).astype(BF)
        return carry

    row_blocks(some_rows)


def upstream_grads(g, level, mods, wo):
    return call(upstream_kernel, (sds((SLOTS, D), BF), sds((SLOTS, HALF), BF)), [VSPEC] * 4)(g, level, mods, wo)


def second_kernel(
    o_own_ref, o_other_ref, h_ref, level_ref, do_ref, embeds_ref, mods_ref, wq, wk, wv, wo,
    dx_ref, h1_ref, y0_ref, x_ref, o_ref, dq_ref, dk_ref, dv_ref,
    q_ref, k_ref, v_ref, lse_ref, ps, dss, bias,
):
    core = lax.axis_index("core")
    bias[...] = fill_bias(level_ref, 1.5)
    own_rows = pl.ds(pl.multiple_of(core * HALF, HALF), HALF)
    other_rows = pl.ds(pl.multiple_of((1 - core) * HALF, HALF), HALF)
    gate0 = mods_ref[2, 0:1, :]
    embed = embeds_ref[1:2, :]
    shift = mods_ref[0, 1:2, :]
    scale = 1.0 + mods_ref[1, 1:2, :]

    def forward_rows(rows):
        y0 = nn(o_own_ref[rows, :], wo[own_rows, :]) + nn(o_other_ref[rows, :], wo[other_rows, :])
        y0_ref[rows, :] = y0.astype(BF)
        h1 = (h_ref[rows, :].astype(F32) + gate0 * y0).astype(BF)
        h1_ref[rows, :] = h1
        factor, normed = norm_rows(h1.astype(F32) + embed)
        x_ref[rows, :] = (normed * scale + shift).astype(BF)

    forward_rows(pl.ds(0, BLK))
    for block in range(NBLK):
        if block + 1 < NBLK:
            forward_rows(pl.ds((block + 1) * BLK, BLK))
        rows = pl.ds(block * BLK, BLK)
        project(x_ref[rows, :], rows, wq, wk, wv, q_ref, k_ref, v_ref)
    attention_forward(q_ref, k_ref, v_ref, o_ref, lse_ref, bias)
    attention_backward(
        q_ref, k_ref, v_ref, o_ref, do_ref, lse_ref, bias, dq_ref, dk_ref, dv_ref, ps, dss
    )

    def backward_rows(rows, carry):
        dx_ref[rows, :] = unproject(rows, wq, wk, wv, dq_ref, dk_ref, dv_ref).astype(BF)
        return carry

    row_blocks(backward_rows)


def second(o_own, o_other, h, level, do, embeds, mods, wq, wk, wv, wo):
    full = sds((SLOTS, D), BF)
    half = sds((SLOTS, HALF), BF)
    scratch = pltpu.VMEM((SLOTS, HALF), BF)
    return call(
        second_kernel,
        (full, full, full, full, half, half, half, half),
        [VSPEC] * 11,
        [
            scratch, scratch, scratch, pltpu.VMEM((8, SLOTS), F32),
            pltpu.VMEM((2, SLOTS, SLOTS), BF), pltpu.VMEM((2, SLOTS, SLOTS), BF),
            pltpu.VMEM((SLOTS, 128), BF),
        ],
        20,
    )(o_own, o_other, h, level, do, embeds, mods, wq, wk, wv, wo)


def sums_kernel(x_ref, o_ref, dy_ref, dq_ref, dk_ref, dv_ref, g_ref, level_ref, wo, grads_ref, gate_ref, grads):
    core = lax.axis_index("core")
    chip = chip_index()
    own_rows = pl.ds(pl.multiple_of(core * HALF, HALF), HALF)

    def some_rows(rows, gate_sum):
        y1 = nn(o_ref[rows, :], wo[own_rows, :])
        deep = jnp.where(level_ref[rows, 0:1] > 1.5, 1.0, 0.0)
        return gate_sum + jnp.sum(g_ref[rows, :].astype(F32) * deep * y1, axis=0, keepdims=True)

    gate_sum = row_blocks(some_rows, jnp.zeros((1, D), F32))
    gate_ref[...] = jnp.broadcast_to(gate_sum, (8, D))
    weight_grads(core, chip, x_ref, o_ref, dy_ref, dq_ref, dk_ref, dv_ref, grads)
    grads_ref[...] = grads[pl.ds(pl.multiple_of((chip % 4) * 32, 32), 32), :]


def second_sums(x, o, dy, dq, dk, dv, g, level, wo):
    return call(
        sums_kernel,
        (sds((32, 5 * HALF), F32), sds((8, D), F32)),
        [VSPEC] * 9,
        [pltpu.VMEM((DH, 5 * HALF), F32)],
    )(x, o, dy, dq, dk, dv, g, level, wo)


def norm_backward(dx, u, scale):
    factor, normed = norm_rows(u)
    shift_sum = jnp.sum(dx, axis=0, keepdims=True)
    scale_sum = jnp.sum(dx * normed, axis=0, keepdims=True)
    dn = dx * scale
    du = factor * (dn - normed * jnp.mean(dn * normed, axis=-1, keepdims=True))
    return du, shift_sum, scale_sum, jnp.sum(du, axis=0, keepdims=True)


def third_kernel(
    dx_own_ref, dx_other_ref, h1_ref, x_ref, g_ref, level_ref, y0_ref,
    q_ref, k_ref, v_ref, o_ref, lse_ref, grads1_ref, gate1_ref, embeds_ref, mods_ref, wo_ref,
    keep_ref, send_ref, mine_ref, sums, dq_ref, dk_ref, dv_ref,
    dy_ref, do_ref, ps, dss, grads, bias, gs,
):
    core = lax.axis_index("core")
    chip = chip_index()
    wo = wo_ref.at[pl.ds(pl.multiple_of(core * HALF, HALF), HALF)]
    bias[...] = fill_bias(level_ref, 0.5)
    gate0 = mods_ref[2, 0:1, :]
    scale1 = 1.0 + mods_ref[1, 1:2, :]
    zero = jnp.zeros((1, D), F32)

    def later_rows(rows, carry):
        shift_sum, scale_sum, embed_sum, gate_sum = carry
        dx = dx_own_ref[rows, :].astype(F32) + dx_other_ref[rows, :].astype(F32)
        u = h1_ref[rows, :].astype(F32) + embeds_ref[1:2, :]
        du, a, b, c = norm_backward(dx, u, scale1)
        shift_sum, scale_sum, embed_sum = shift_sum + a, scale_sum + b, embed_sum + c
        g = g_ref[rows, :].astype(F32) + du
        gs[rows, :] = g
        gate_sum += jnp.sum(g * y0_ref[rows, :].astype(F32), axis=0, keepdims=True)
        dy = (g * gate0).astype(BF)
        dy_ref[rows, :] = dy
        do_ref[rows, :] = nt(dy, wo[...]).astype(BF)
        return shift_sum, scale_sum, embed_sum, gate_sum

    carry = row_blocks(later_rows, (zero,) * 4)
    shift_sum, scale_sum, embed_sum, gate_sum = carry
    sums[...] = jnp.zeros((8, D), F32)
    sums[2:3, :] = 0.5 * gate_sum
    sums[3:4, :] = 0.5 * shift_sum
    sums[4:5, :] = 0.5 * scale_sum
    sums[5:6, :] = gate1_ref[0:1, :]
    sums[7:8, :] = 0.5 * embed_sum
    attention_backward(
        q_ref, k_ref, v_ref, o_ref, do_ref, lse_ref, bias, dq_ref, dk_ref, dv_ref, ps, dss
    )
    weight_grads(core, chip, x_ref, o_ref, dy_ref, dq_ref, dk_ref, dv_ref, grads)
    base = pl.multiple_of((chip % 4) * 32, 32)
    mine16 = pl.ds(pl.multiple_of(core * 16, 16), 16)
    other16 = pl.ds(pl.multiple_of((1 - core) * 16, 16), 16)
    chip_grads = grads.at[pl.ds(base, 32)]
    keep_ref[...] = (chip_grads[mine16, :] + grads1_ref[mine16, :]).astype(BF)
    send_ref[...] = (chip_grads[other16, :] + grads1_ref[other16, :]).astype(BF)
    g_rows = gs.at[pl.ds(pl.multiple_of(chip * 2 * CAP, 8), 2 * CAP)]
    mine_ref[...] = jnp.where(core == 0, g_rows[0:CAP, :], g_rows[CAP : 2 * CAP, :])


def third(dx_own, dx_other, h1, x, g, level, y0, q, k, v, o, lse, grads1, gate1, embeds, mods, wo):
    packed = sds((16, 5 * HALF), BF)
    half = sds((SLOTS, HALF), BF)
    return call(
        third_kernel,
        (packed, packed, sds((CAP, D), F32), sds((8, D), F32), half, half, half),
        [VSPEC] * 17,
        [
            pltpu.VMEM((SLOTS, D), BF), pltpu.VMEM((SLOTS, HALF), BF),
            pltpu.VMEM((2, SLOTS, SLOTS), BF), pltpu.VMEM((2, SLOTS, SLOTS), BF),
            pltpu.VMEM((DH, 5 * HALF), F32), pltpu.VMEM((SLOTS, 128), BF), pltpu.VMEM((SLOTS, D), F32),
        ],
        24,
    )(dx_own, dx_other, h1, x, g, level, y0, q, k, v, o, lse, grads1, gate1, embeds, mods, wo)


def last_kernel(
    dq_ref, dk_ref, dv_ref, h_ref, sums1_ref, embeds_ref, mods_ref, wq, wk, wv,
    keep_ref, send_ref, dx0, sums,
):
    core = lax.axis_index("core")
    chip = chip_index()
    scale0 = 1.0 + mods_ref[1, 0:1, :]
    zero = jnp.zeros((1, D), F32)

    def unproject_rows(block):
        rows = pl.ds(block * BLK, BLK)
        dx0[rows, :] = unproject(rows, wq, wk, wv, dq_ref, dk_ref, dv_ref)

    def earlier_rows(block, carry):
        shift_sum, scale_sum, embed_sum = carry
        rows = pl.ds(block * BLK, BLK)
        dx = dx0[rows, :]
        u = h_ref[rows, :].astype(F32) + embeds_ref[0:1, :]
        du, a, b, c = norm_backward(dx, u, scale0)
        return shift_sum + a, scale_sum + b, embed_sum + c

    carry = (zero,) * 3
    unproject_rows(0)
    for block in range(NBLK):
        if block + 1 < NBLK:
            unproject_rows(block + 1)
        carry = earlier_rows(block, carry)
    shift_sum, scale_sum, embed_sum = carry
    sums[...] = sums1_ref[...]
    sums[0:1, :] = shift_sum
    sums[1:2, :] = scale_sum
    sums[6:7, :] = embed_sum
    total = jnp.concatenate([sums[:, 0:HALF], sums[:, HALF:D]], axis=0).astype(BF)
    keep_ref[:, 0:HALF] = total
    send_ref[:, 0:HALF] = total
    first_half = core == 0
    chip_rows = dx0.at[pl.ds(pl.multiple_of(chip * 2 * CAP, 8), 2 * CAP)]
    lower = chip_rows[0:16, :]
    upper = chip_rows[CAP - 4 : 2 * CAP, :]
    upper = jnp.concatenate([upper[4:16], upper[0:4]], axis=0)
    keep_ref[:, HALF : 3 * HALF] = jnp.where(first_half, lower, upper).astype(BF)
    send_ref[:, HALF : 3 * HALF] = jnp.where(first_half, upper, lower).astype(BF)


def last(dq, dk, dv, h, sums1, embeds, mods, wq, wk, wv):
    packed = sds((16, 3 * HALF), BF)
    return call(
        last_kernel,
        (packed, packed),
        [VSPEC] * 10,
        [pltpu.VMEM((SLOTS, D), F32), pltpu.VMEM((8, D), F32)],
        16,
    )(dq, dk, dv, h, sums1, embeds, mods, wq, wk, wv)


def join_kernel(keep_ref, other_ref, left_ref, right_ref):
    core = lax.axis_index("core")
    for part, (out, start) in enumerate(((left_ref, 0), (left_ref, D), (right_ref, 0))):
        cols = slice(part * HALF, (part + 1) * HALF)
        out[:, pl.ds(pl.multiple_of(start + core * HALF, HALF), HALF)] = keep_ref[:, cols]
        out[:, pl.ds(pl.multiple_of(start + (1 - core) * HALF, HALF), HALF)] = other_ref[:, cols]
    shared = slice(3 * HALF, 5 * HALF)
    both = keep_ref[:, shared].astype(F32) + other_ref[:, shared].astype(F32)
    right_ref[:, D : 2 * D] = both.astype(BF)


def join(keep, other):
    half = sds((16, 2 * D), BF)
    return call(join_kernel, (half, half), [VSPEC, VSPEC])(keep, other)


def total_kernel(keep_ref, other_ref, out_ref):
    both = keep_ref[:, 0:HALF].astype(F32) + other_ref[:, 0:HALF].astype(F32)
    out_ref[...] = both.astype(BF)


def total(keep, other):
    return call(total_kernel, (sds((16, HALF), BF),), [VSPEC, VSPEC])(keep, other)[0]


def hidden_kernel(keep_ref, other_ref, mine_ref, rows_ref, picker_ref, cot_ref, embeds_ref, mods_ref, out_ref):
    cols = slice(HALF, 3 * HALF)
    dx = keep_ref[:, cols].astype(F32) + other_ref[:, cols].astype(F32)
    dx = dx[0:CAP]
    factor, normed = norm_rows(rows_ref[...].astype(F32)[0:CAP] + embeds_ref[0:1, :])
    dn = dx * (1.0 + mods_ref[1, 0:1, :])
    du = factor * (dn - normed * jnp.mean(dn * normed, axis=-1, keepdims=True))
    rows = jnp.concatenate([mine_ref[...] + du, jnp.zeros((16 - CAP, D), F32)], axis=0).astype(BF)
    picker = picker_ref[...]
    placed = tn(picker, rows)
    taken = tn(picker, jnp.ones((16, 128), BF))
    taken = jnp.concatenate([taken] * 8, axis=1)
    out_ref[0] = jnp.where(taken > 0.5, placed.astype(BF), cot_ref[0])


def hidden_grad(keep, other, mine, rows, picker, cot, embeds, mods):
    specs = [VSPEC] * 5 + [LOAD] + [VSPEC] * 2
    return call(hidden_kernel, (sds((1, TOK, D), BF),), specs, pinned=False)(
        keep, other, mine, rows, picker, cot, embeds, mods
    )[0]


def swap_cores(x):
    return lax.ppermute(x, "core", [(0, 1), (1, 0)])


def chip_index():
    return (lax.axis_index("zl") * 4 + lax.axis_index("x")) * 4 + lax.axis_index("y")


def sequence_work(gathered, rows, picker, cot, embeds, mods, weights):
    wq, wk, wv, wo = weights
    mods = mods.transpose(1, 0, 2)
    other = swap_cores(gathered)
    q, k, v, o, lse, h, g, level, x, wq, wk, wv, wo = first(gathered, other, embeds, mods, wq, wk, wv, wo)
    o_other = swap_cores(o)
    dy1, do1 = upstream_grads(g, level, mods, wo)
    dx, h1, y0, x1, o1, dq1, dk1, dv1 = second(o, o_other, h, level, do1, embeds, mods, wq, wk, wv, wo)
    dx_other = swap_cores(dx)
    grads1, gate1 = second_sums(x1, o1, dy1, dq1, dk1, dv1, g, level, wo)
    keep, send, mine, sums1, dq0, dk0, dv0 = third(
        dx, dx_other, h1, x, g, level, y0, q, k, v, o, lse, grads1, gate1, embeds, mods, wo
    )
    left, right = join(keep, swap_cores(send))
    keep_rows, send_rows = last(dq0, dk0, dv0, h, sums1, embeds, mods, wq, wk, wv)
    other_rows = swap_cores(send_rows)
    hidden = hidden_grad(keep_rows, other_rows, mine, rows, picker, cot, embeds, mods)
    return left, right, total(keep_rows, other_rows), hidden


def pair_kernel(left_ref, left_other_ref, right_ref, right_other_ref, sums_ref, sums_other_ref, left_out, right_out):
    left_out[:, 0 : 2 * D] = (left_ref[...].astype(F32) + left_other_ref[...].astype(F32)).astype(BF)
    left_out[:, 2 * D :] = (sums_ref[...].astype(F32) + sums_other_ref[...].astype(F32)).astype(BF)
    right_out[...] = (right_ref[...].astype(F32) + right_other_ref[...].astype(F32)).astype(BF)


def final_kernel(
    left_ref, left_other_ref, right_ref, right_other_ref,
    gq_ref, gk_ref, gv_ref, go_ref, embeds_ref, mods_ref,
):
    left = left_ref[...].astype(F32) + left_other_ref[...].astype(F32)
    right = right_ref[...].astype(F32) + right_other_ref[...].astype(F32)
    gq_ref[...] = left[:, 0:D]
    gk_ref[...] = left[:, D : 2 * D]
    gv_ref[...] = right[:, 0:D]
    go_ref[...] = right[:, D : 2 * D]
    sums = jnp.concatenate([left[0:8, 2 * D :], left[8:16, 2 * D :]], axis=1)
    for kind in range(3):
        for section in range(2):
            row = 3 * section + kind
            mods_ref[kind, section : section + 1, :] = sums[row : row + 1]
    embeds_ref[...] = sums[6:8]


def dp_sum(left, right, sums):
    def swap(x, far):
        return lax.ppermute(x, "dp", [(i, i ^ far) for i in range(4)])

    left, right = call(pair_kernel, (sds((16, 2 * D + HALF), BF), sds((16, 2 * D), BF)), [VSPEC] * 6)(
        left, swap(left, 1), right, swap(right, 3), sums, swap(sums, 1)
    )
    block = sds((16, D), F32)
    return call(
        final_kernel,
        (block, block, block, block, sds((2, D), F32), sds((3, 2, D), F32)),
        [VSPEC] * 4,
        pinned=False,
    )(left, swap(left, 3), right, swap(right, 1))


def shards(hidden, depth, cotangent, embeds, mods, w_query, w_key, w_value, w_out):
    payload, picker, rows = pick(depth, hidden, cotangent)
    spread = jnp.broadcast_to(payload[None], (CHIPS, PACKED, 128))
    gathered = lax.all_to_all(spread, ("zl", "x", "y"), 0, 0, tiled=True)
    left, right, sums, grad_hidden = sequence_work(
        gathered, rows, picker, cotangent, embeds, mods, (w_query, w_key, w_value, w_out)
    )
    gq, gk, gv, go, grad_embeds, grad_mods = dp_sum(left, right, sums)
    return (grad_hidden, gq, gk, gv, go, grad_embeds, grad_mods.transpose(1, 0, 2))


def solution(mesh):
    split = Mesh(mesh.devices.reshape(2, 4, 4, 2, 4), ("zl", "x", "y", "core", "dp"))
    ctx = ("zl", "x", "y", "core")
    in_specs = (P("dp", ctx, None), P("dp", ctx), P("dp", ctx, None)) + (P(),) * 6
    out_specs = (P("dp", ctx, None),) + (P(ctx, None),) * 4 + (P(), P())
    return jax.shard_map(shards, mesh=split, in_specs=in_specs, out_specs=out_specs, check_vma=False)
```

```python
import jax
import jax.numpy as jnp
from jax import lax
from jax.experimental import pallas as pl
from jax.experimental.pallas import tpu as pltpu
from jax.sharding import Mesh, PartitionSpec as P

D = 1024
H = 8
DH = 128
TOK = 128
CAP = 12
N_CTX = 64
CHIPS = 32
SLOTS = 768
HALF = 512
HEADS = 4
FORWARD_HEADS = 4
BACKWARD_HEADS = 4
TILES = 24
PACKED = (TILES + 1) * 8
BLK = 256
NBLK = SLOTS // BLK
EPSILON = 1e-06
NEGATIVE = -1e30
EMPTY = 64.0
SCALE = DH ** (-0.5)
SCALE2 = SCALE * 1.4426950408889634
BF = jnp.bfloat16
F32 = jnp.float32

VSPEC = pl.BlockSpec(memory_space=pltpu.VMEM)
LOAD = pl.BlockSpec(memory_space=pltpu.VMEM)
HSPEC = pl.BlockSpec(memory_space=pl.ANY)


def nn(a, b):
    return lax.dot_general(a, b, (((1,), (0,)), ((), ())), preferred_element_type=F32)


def nt(a, b):
    return lax.dot_general(a, b, (((1,), (1,)), ((), ())), preferred_element_type=F32)


def tn(a, b):
    return lax.dot_general(a, b, (((0,), (0,)), ((), ())), preferred_element_type=F32)


def sds(shape, dtype):
    return jax.ShapeDtypeStruct(shape, dtype)


def call(kernel, outs, in_specs, scratch=(), vmem=16, pinned=True):
    if pinned:
        outs = tuple(pltpu.VMEM(s.shape, s.dtype) for s in outs)
    run = pl.pallas_call(
        kernel,
        out_shape=outs,
        in_specs=in_specs,
        out_specs=tuple(VSPEC for _ in outs),
        scratch_shapes=list(scratch),
        compiler_params=pltpu.CompilerParams(vmem_limit_bytes=vmem * 1024 * 1024),
    )

    def placed(*args):
        spaces = [pltpu.VMEM if spec is VSPEC else pltpu.HBM for spec in in_specs]
        return run(*(pltpu.with_memory_space_constraint(a, m) for a, m in zip(args, spaces)))

    return placed


def pick_kernel(depth_ref, hidden_ref, cot_ref, payload_ref, picker_ref, rows_ref, both):
    depth = jnp.broadcast_to(depth_ref[...], (16, TOK))
    active = depth >= 2
    before = lax.broadcasted_iota(jnp.int32, (TOK, TOK), 0)
    upto = lax.broadcasted_iota(jnp.int32, (TOK, TOK), 1)
    upper = jnp.where(before <= upto, 1.0, 0.0).astype(BF)
    placing = nn(jnp.where(active, 1.0, 0.0).astype(BF), upper) - 1.0
    slot = lax.broadcasted_iota(jnp.int32, (16, TOK), 0)
    hit = active & (placing == slot.astype(F32)) & (slot < CAP)
    picker = jnp.where(hit, 1.0, 0.0)
    picker_ref[...] = picker.astype(BF)
    level = jnp.sum(picker * (depth - 1).astype(F32), axis=1, keepdims=True)
    rows = nn(picker.astype(BF), hidden_ref[0])
    both[0:CAP] = jnp.where(level > 0.5, rows, EMPTY)[0:CAP]
    both[CAP : 2 * CAP] = nn(picker.astype(BF), cot_ref[0])[0:CAP]
    lane = lax.broadcasted_iota(jnp.int32, (8, 128), 1)
    level = jnp.broadcast_to(level, (16, 128))
    tiles = [both[8 * r : 8 * r + 8, 128 * c : 128 * c + 128] for r in range(3) for c in range(8)]
    tiles.append(jnp.where(lane < 64, level[0:8], level[8:16]))
    payload_ref[...] = jnp.concatenate(tiles, axis=0).astype(BF)
    rows_ref[...] = both[0:16].astype(BF)


def pick(depth, hidden, cotangent):
    return call(
        pick_kernel,
        (sds((PACKED, 128), BF), sds((16, TOK), BF), sds((16, D), BF)),
        [LOAD, LOAD, LOAD],
        [pltpu.VMEM((2 * CAP, D), F32)],
    )(depth, hidden, cotangent)


def causal_bias():
    key = lax.broadcasted_iota(jnp.int32, (BLK, BLK), 0)
    query = lax.broadcasted_iota(jnp.int32, (BLK, BLK), 1)
    return jnp.where(key <= query, 0.0, NEGATIVE).astype(F32)


def fill_bias(level_ref, least):
    lane = lax.broadcasted_iota(jnp.int32, (SLOTS, DH), 1)
    return jnp.where((level_ref[...] > least) | (lane > 0), 0.0, NEGATIVE).astype(BF)


def norm_rows(u):
    factor = lax.rsqrt(jnp.mean(u * u, axis=-1, keepdims=True) + EPSILON)
    return factor, u * factor


def biased_scores(k, q, bias_ref, causal, upto):
    lane = lax.broadcasted_iota(jnp.int32, (BLK, DH), 1)
    unit = jnp.where(lane == 0, 1.0, 0.0).astype(BF)
    s = nt(jnp.concatenate([k, bias_ref[0:upto, :]], axis=1), jnp.concatenate([q, unit], axis=1))
    last = s[upto - BLK : upto] + causal
    if upto == BLK:
        return last
    return jnp.concatenate([s[: upto - BLK], last], axis=0)


def row_blocks(body, carry=0):
    def step(block, carry):
        return body(pl.ds(pl.multiple_of(block * BLK, BLK), BLK), carry)

    return lax.fori_loop(0, NBLK, step, carry)


def head_cols(head):
    return pl.ds(pl.multiple_of(head * DH, DH), DH)


def attention_forward(q_ref, k_ref, v_ref, o_ref, lse_ref, bias_ref):
    causal = causal_bias()
    ones = jnp.ones((16, SLOTS), BF)

    def some_heads(step, carry):
        items = []
        for part in range(FORWARD_HEADS):
            head = step * FORWARD_HEADS + part
            cols = head_cols(head)
            vt = jnp.concatenate([v_ref[:, cols].T, ones], axis=0)
            items += [(head, cols, vt, block) for block in range(NBLK)]

        def start(head, cols, vt, block):
            upto = (block + 1) * BLK
            s = biased_scores(k_ref[0:upto, cols], q_ref[block * BLK : upto, cols], bias_ref, causal, upto)
            return s, jnp.max(s, axis=0, keepdims=True)

        def finish(head, cols, vt, block, s, top):
            upto = (block + 1) * BLK
            rows = slice(block * BLK, upto)
            e = jnp.exp2((s - top) * SCALE2).astype(BF)
            both = nn(vt[:, 0:upto], e)
            total = both[DH : DH + 1]
            o_ref[rows, cols] = (both[0:DH] * (1.0 / total)).T.astype(BF)
            lse_ref[pl.ds(head, 1), rows] = jnp.maximum(top * SCALE2 + jnp.log2(total), -1e25)

        states = [start(*item) for item in items[:2]]
        for i, item in enumerate(items):
            if i + 2 < len(items):
                states.append(start(*items[i + 2]))
            finish(*item, *states[i])
        return carry

    lax.fori_loop(0, HEADS // FORWARD_HEADS, some_heads, 0)


def attention_backward(
    q_ref, k_ref, v_ref, o_ref, do_ref, lse_ref, bias_ref, dq_ref, dk_ref, dv_ref, ps, dss
):
    causal = causal_bias()

    def some_heads(step, carry):
        items = []
        for part in range(BACKWARD_HEADS):
            head = step * BACKWARD_HEADS + part
            cols = head_cols(head)
            kt = k_ref[:, cols].T
            items += [(head, part % 2, cols, kt, block) for block in range(NBLK)]

        def start(head, slot, cols, kt, block):
            upto = (block + 1) * BLK
            rows = slice(block * BLK, upto)
            s = biased_scores(k_ref[0:upto, cols], q_ref[rows, cols], bias_ref, causal, upto)
            return s, nt(v_ref[0:upto, cols], do_ref[rows, cols])

        def finish(head, slot, cols, kt, block, s, dp):
            upto = (block + 1) * BLK
            rows = slice(block * BLK, upto)
            product = do_ref[rows, cols].astype(F32) * o_ref[rows, cols].astype(F32)
            inner = jnp.sum(product.T, axis=0, keepdims=True)
            p = jnp.exp2(s * SCALE2 - lse_ref[pl.ds(head, 1), rows])
            ds = (p * (dp - inner)).astype(BF)
            ps[slot, 0:upto, rows] = p.astype(BF)
            dss[slot, 0:upto, rows] = ds
            dq_ref[rows, cols] = (nn(kt[:, 0:upto], ds).T * SCALE).astype(BF)

        def close(head, slot, cols):
            for block in range(NBLK):
                rows = slice(block * BLK, (block + 1) * BLK)
                later = slice(block * BLK, SLOTS)
                dv_ref[rows, cols] = nn(ps[slot, rows, later], do_ref[later, cols]).astype(BF)
                dk_ref[rows, cols] = (nn(dss[slot, rows, later], q_ref[later, cols]) * SCALE).astype(BF)

        states = [start(*item) for item in items[:1]]
        for i, item in enumerate(items):
            if i + 1 < len(items):
                states.append(start(*items[i + 1]))
            finish(*item, *states[i])
            if item[-1] == NBLK - 1:
                close(*item[:3])
        return carry

    lax.fori_loop(0, HEADS // BACKWARD_HEADS, some_heads, 0)


def project(x, rows, wq, wk, wv, q_ref, k_ref, v_ref):
    q_ref[rows, :] = nn(x, wq[...]).astype(BF)
    k_ref[rows, :] = nn(x, wk[...]).astype(BF)
    v_ref[rows, :] = nn(x, wv[...]).astype(BF)


def unproject(rows, wq, wk, wv, dq_ref, dk_ref, dv_ref):
    return nt(dq_ref[rows, :], wq[...]) + nt(dk_ref[rows, :], wk[...]) + nt(dv_ref[rows, :], wv[...])


def place_block(block_ref, chip, base, start, hs, gs, level):
    tiles = block_ref[chip].astype(F32)
    rows_h = hs.at[pl.ds(base, 2 * CAP)]
    rows_g = gs.at[pl.ds(base, 2 * CAP)]
    rows_level = level.at[pl.ds(base, 2 * CAP)]
    for c in range(8):
        cols = slice(128 * c, 128 * c + 128)
        upper, middle, lower = (tiles[8 * (8 * r + c) : 8 * (8 * r + c) + 8] for r in range(3))
        rows_h[start : start + 8, cols] = upper
        rows_h[start + 8 : start + 12, cols] = middle[0:4]
        rows_g[start : start + 4, cols] = middle[4:8]
        rows_g[start + 4 : start + 12, cols] = lower
    depths = tiles[8 * TILES :]
    turned = pltpu.roll(depths, 64, 1)
    lane = lax.broadcasted_iota(jnp.int32, (8, 128), 1)
    rows_level[start : start + 8] = jnp.where(lane < 64, depths, turned)
    rows_level[start + 8 : start + 12] = jnp.where(lane < 64, turned, depths)[0:4]


def weight_grads(core, chip, x_ref, o_ref, dy_ref, dq_ref, dk_ref, dv_ref, grads):
    strip = pl.multiple_of((chip // 4) * DH, DH)
    xs = x_ref[:, pl.ds(strip, DH)]
    grads[:, 0:HALF] = tn(xs, dq_ref[...])
    grads[:, HALF : 2 * HALF] = tn(xs, dk_ref[...])
    grads[:, 2 * HALF : 3 * HALF] = tn(xs, dv_ref[...])
    own = jnp.where(chip // 16 == core, 1.0, 0.0).astype(F32)
    o_strip = pl.multiple_of(((chip // 4) % 4) * DH, DH)
    os = o_ref[:, pl.ds(o_strip, DH)]
    grads[:, 3 * HALF :] = tn(os, dy_ref[...]) * own


def first_kernel(
    own_ref, other_ref, embeds_ref, mods_ref, wq_hbm, wk_hbm, wv_hbm, wo_hbm,
    q_ref, k_ref, v_ref, o_ref, lse_ref, h_ref, g_ref, level_ref, x_ref, wq, wk, wv, wo,
    hs, gs, bias, sems,
):
    core = lax.axis_index("core")
    half = pl.ds(pl.multiple_of(core * HALF, HALF), HALF)
    copies = [
        pltpu.make_async_copy(source.at[:, half], target, sems.at[i])
        for i, (source, target) in enumerate(((wq_hbm, wq), (wk_hbm, wk), (wv_hbm, wv)))
    ]
    copies.append(pltpu.make_async_copy(wo_hbm, wo, sems.at[3]))
    for copy in copies:
        copy.start()

    def place(even_ref, odd_ref):
        def one_chip(chip, carry):
            base = pl.multiple_of(chip * 2 * CAP, 8)
            place_block(even_ref, chip, base, 0, hs, gs, level_ref)
            place_block(odd_ref, chip, base, CAP, hs, gs, level_ref)
            return carry

        lax.fori_loop(0, CHIPS, one_chip, 0, unroll=4)

    @pl.when(core == 0)
    def _():
        place(own_ref, other_ref)

    @pl.when(core == 1)
    def _():
        place(other_ref, own_ref)

    bias[...] = fill_bias(level_ref, 0.5)
    for copy in copies:
        copy.wait()
    embed = embeds_ref[0:1, :]
    shift = mods_ref[0, 0:1, :]
    scale = 1.0 + mods_ref[1, 0:1, :]

    def norm_block(rows):
        h = hs[rows, :]
        g_ref[rows, :] = gs[rows, :].astype(BF)
        h_ref[rows, :] = h.astype(BF)
        factor, normed = norm_rows(h + embed)
        x_ref[rows, :] = (normed * scale + shift).astype(BF)

    norm_block(pl.ds(0, BLK))
    for block in range(NBLK):
        if block + 1 < NBLK:
            norm_block(pl.ds((block + 1) * BLK, BLK))
        rows = pl.ds(block * BLK, BLK)
        project(x_ref[rows, :], rows, wq, wk, wv, q_ref, k_ref, v_ref)
    attention_forward(q_ref, k_ref, v_ref, o_ref, lse_ref, bias)


def first(own, other, embeds, mods, wq, wk, wv, wo):
    half = sds((SLOTS, HALF), BF)
    full = sds((SLOTS, D), BF)
    return call(
        first_kernel,
        (half, half, half, half, sds((8, SLOTS), F32), full, full, sds((SLOTS, 128), F32), full)
        + (sds((D, HALF), BF),) * 3
        + (sds((D, D), BF),),
        [VSPEC] * 4 + [HSPEC] * 4,
        [
            pltpu.VMEM((SLOTS, D), F32),
            pltpu.VMEM((SLOTS, D), F32),
            pltpu.VMEM((SLOTS, 128), BF),
            pltpu.SemaphoreType.DMA((4,)),
        ],
        16,
    )(own, other, embeds, mods, wq, wk, wv, wo)


def upstream_kernel(g_ref, level_ref, mods_ref, wo, dy_ref, do_ref):
    core = lax.axis_index("core")
    own_rows = pl.ds(pl.multiple_of(core * HALF, HALF), HALF)
    gate1 = mods_ref[2, 1:2, :]

    def some_rows(rows, carry):
        deep = jnp.where(level_ref[rows, 0:1] > 1.5, 1.0, 0.0)
        dy = (g_ref[rows, :].astype(F32) * deep * gate1).astype(BF)
        dy_ref[rows, :] = dy
        do_ref[rows, :] = nt(dy, wo[own_rows, :]).astype(BF)
        return carry

    row_blocks(some_rows)


def upstream_grads(g, level, mods, wo):
    return call(upstream_kernel, (sds((SLOTS, D), BF), sds((SLOTS, HALF), BF)), [VSPEC] * 4)(g, level, mods, wo)


def second_kernel(
    o_own_ref, o_other_ref, h_ref, level_ref, do_ref, embeds_ref, mods_ref, wq, wk, wv, wo,
    dx_ref, h1_ref, y0_ref, x_ref, o_ref, dq_ref, dk_ref, dv_ref,
    q_ref, k_ref, v_ref, lse_ref, ps, dss, bias,
):
    core = lax.axis_index("core")
    bias[...] = fill_bias(level_ref, 1.5)
    own_rows = pl.ds(pl.multiple_of(core * HALF, HALF), HALF)
    other_rows = pl.ds(pl.multiple_of((1 - core) * HALF, HALF), HALF)
    gate0 = mods_ref[2, 0:1, :]
    embed = embeds_ref[1:2, :]
    shift = mods_ref[0, 1:2, :]
    scale = 1.0 + mods_ref[1, 1:2, :]

    def forward_rows(rows):
        y0 = nn(o_own_ref[rows, :], wo[own_rows, :]) + nn(o_other_ref[rows, :], wo[other_rows, :])
        y0_ref[rows, :] = y0.astype(BF)
        h1 = (h_ref[rows, :].astype(F32) + gate0 * y0).astype(BF)
        h1_ref[rows, :] = h1
        factor, normed = norm_rows(h1.astype(F32) + embed)
        x_ref[rows, :] = (normed * scale + shift).astype(BF)

    forward_rows(pl.ds(0, BLK))
    for block in range(NBLK):
        if block + 1 < NBLK:
            forward_rows(pl.ds((block + 1) * BLK, BLK))
        rows = pl.ds(block * BLK, BLK)
        project(x_ref[rows, :], rows, wq, wk, wv, q_ref, k_ref, v_ref)
    attention_forward(q_ref, k_ref, v_ref, o_ref, lse_ref, bias)
    attention_backward(
        q_ref, k_ref, v_ref, o_ref, do_ref, lse_ref, bias, dq_ref, dk_ref, dv_ref, ps, dss
    )

    for block in range(NBLK):
        rows = pl.ds(block * BLK, BLK)
        dx_ref[rows, :] = unproject(rows, wq, wk, wv, dq_ref, dk_ref, dv_ref).astype(BF)


def second(o_own, o_other, h, level, do, embeds, mods, wq, wk, wv, wo):
    full = sds((SLOTS, D), BF)
    half = sds((SLOTS, HALF), BF)
    scratch = pltpu.VMEM((SLOTS, HALF), BF)
    return call(
        second_kernel,
        (full, full, full, full, half, half, half, half),
        [VSPEC] * 11,
        [
            scratch, scratch, scratch, pltpu.VMEM((8, SLOTS), F32),
            pltpu.VMEM((2, SLOTS, SLOTS), BF), pltpu.VMEM((2, SLOTS, SLOTS), BF),
            pltpu.VMEM((SLOTS, 128), BF),
        ],
        20,
    )(o_own, o_other, h, level, do, embeds, mods, wq, wk, wv, wo)


def sums_kernel(x_ref, o_ref, dy_ref, dq_ref, dk_ref, dv_ref, g_ref, level_ref, wo, grads_ref, gate_ref, grads):
    core = lax.axis_index("core")
    chip = chip_index()
    own_rows = pl.ds(pl.multiple_of(core * HALF, HALF), HALF)

    def some_rows(rows, gate_sum):
        y1 = nn(o_ref[rows, :], wo[own_rows, :])
        deep = jnp.where(level_ref[rows, 0:1] > 1.5, 1.0, 0.0)
        return gate_sum + jnp.sum(g_ref[rows, :].astype(F32) * deep * y1, axis=0, keepdims=True)

    gate_sum = row_blocks(some_rows, jnp.zeros((1, D), F32))
    gate_ref[...] = jnp.broadcast_to(gate_sum, (8, D))
    weight_grads(core, chip, x_ref, o_ref, dy_ref, dq_ref, dk_ref, dv_ref, grads)
    grads_ref[...] = grads[pl.ds(pl.multiple_of((chip % 4) * 32, 32), 32), :]


def second_sums(x, o, dy, dq, dk, dv, g, level, wo):
    return call(
        sums_kernel,
        (sds((32, 5 * HALF), F32), sds((8, D), F32)),
        [VSPEC] * 9,
        [pltpu.VMEM((DH, 5 * HALF), F32)],
    )(x, o, dy, dq, dk, dv, g, level, wo)


def norm_backward(dx, u, scale):
    factor, normed = norm_rows(u)
    shift_sum = jnp.sum(dx, axis=0, keepdims=True)
    scale_sum = jnp.sum(dx * normed, axis=0, keepdims=True)
    dn = dx * scale
    du = factor * (dn - normed * jnp.mean(dn * normed, axis=-1, keepdims=True))
    return du, shift_sum, scale_sum, jnp.sum(du, axis=0, keepdims=True)


def third_kernel(
    dx_own_ref, dx_other_ref, h1_ref, x_ref, g_ref, level_ref, y0_ref,
    q_ref, k_ref, v_ref, o_ref, lse_ref, grads1_ref, gate1_ref, embeds_ref, mods_ref, wo_ref,
    keep_ref, send_ref, mine_ref, sums, dq_ref, dk_ref, dv_ref,
    dy_ref, do_ref, ps, dss, grads, bias, gs,
):
    core = lax.axis_index("core")
    chip = chip_index()
    wo = wo_ref.at[pl.ds(pl.multiple_of(core * HALF, HALF), HALF)]
    bias[...] = fill_bias(level_ref, 0.5)
    gate0 = mods_ref[2, 0:1, :]
    scale1 = 1.0 + mods_ref[1, 1:2, :]
    zero = jnp.zeros((1, D), F32)

    def later_rows(rows, carry):
        shift_sum, scale_sum, embed_sum, gate_sum = carry
        dx = dx_own_ref[rows, :].astype(F32) + dx_other_ref[rows, :].astype(F32)
        u = h1_ref[rows, :].astype(F32) + embeds_ref[1:2, :]
        du, a, b, c = norm_backward(dx, u, scale1)
        shift_sum, scale_sum, embed_sum = shift_sum + a, scale_sum + b, embed_sum + c
        g = g_ref[rows, :].astype(F32) + du
        gs[rows, :] = g
        gate_sum += jnp.sum(g * y0_ref[rows, :].astype(F32), axis=0, keepdims=True)
        dy = (g * gate0).astype(BF)
        dy_ref[rows, :] = dy
        do_ref[rows, :] = nt(dy, wo[...]).astype(BF)
        return shift_sum, scale_sum, embed_sum, gate_sum

    carry = row_blocks(later_rows, (zero,) * 4)
    shift_sum, scale_sum, embed_sum, gate_sum = carry
    sums[...] = jnp.zeros((8, D), F32)
    sums[2:3, :] = 0.5 * gate_sum
    sums[3:4, :] = 0.5 * shift_sum
    sums[4:5, :] = 0.5 * scale_sum
    sums[5:6, :] = gate1_ref[0:1, :]
    sums[7:8, :] = 0.5 * embed_sum
    attention_backward(
        q_ref, k_ref, v_ref, o_ref, do_ref, lse_ref, bias, dq_ref, dk_ref, dv_ref, ps, dss
    )
    weight_grads(core, chip, x_ref, o_ref, dy_ref, dq_ref, dk_ref, dv_ref, grads)
    base = pl.multiple_of((chip % 4) * 32, 32)
    mine16 = pl.ds(pl.multiple_of(core * 16, 16), 16)
    other16 = pl.ds(pl.multiple_of((1 - core) * 16, 16), 16)
    chip_grads = grads.at[pl.ds(base, 32)]
    keep_ref[...] = (chip_grads[mine16, :] + grads1_ref[mine16, :]).astype(BF)
    send_ref[...] = (chip_grads[other16, :] + grads1_ref[other16, :]).astype(BF)
    g_rows = gs.at[pl.ds(pl.multiple_of(chip * 2 * CAP, 8), 2 * CAP)]
    mine_ref[...] = jnp.where(core == 0, g_rows[0:CAP, :], g_rows[CAP : 2 * CAP, :])


def third(dx_own, dx_other, h1, x, g, level, y0, q, k, v, o, lse, grads1, gate1, embeds, mods, wo):
    packed = sds((16, 5 * HALF), BF)
    half = sds((SLOTS, HALF), BF)
    return call(
        third_kernel,
        (packed, packed, sds((CAP, D), F32), sds((8, D), F32), half, half, half),
        [VSPEC] * 17,
        [
            pltpu.VMEM((SLOTS, D), BF), pltpu.VMEM((SLOTS, HALF), BF),
            pltpu.VMEM((2, SLOTS, SLOTS), BF), pltpu.VMEM((2, SLOTS, SLOTS), BF),
            pltpu.VMEM((DH, 5 * HALF), F32), pltpu.VMEM((SLOTS, 128), BF), pltpu.VMEM((SLOTS, D), F32),
        ],
        24,
    )(dx_own, dx_other, h1, x, g, level, y0, q, k, v, o, lse, grads1, gate1, embeds, mods, wo)


def last_kernel(
    dq_ref, dk_ref, dv_ref, h_ref, sums1_ref, embeds_ref, mods_ref, wq, wk, wv,
    keep_ref, send_ref, dx0, sums,
):
    core = lax.axis_index("core")
    chip = chip_index()
    scale0 = 1.0 + mods_ref[1, 0:1, :]
    zero = jnp.zeros((1, D), F32)

    def unproject_rows(block):
        rows = pl.ds(block * BLK, BLK)
        dx0[rows, :] = unproject(rows, wq, wk, wv, dq_ref, dk_ref, dv_ref)

    def earlier_rows(block, carry):
        shift_sum, scale_sum, embed_sum = carry
        rows = pl.ds(block * BLK, BLK)
        dx = dx0[rows, :]
        u = h_ref[rows, :].astype(F32) + embeds_ref[0:1, :]
        du, a, b, c = norm_backward(dx, u, scale0)
        return shift_sum + a, scale_sum + b, embed_sum + c

    carry = (zero,) * 3
    unproject_rows(0)
    for block in range(NBLK):
        if block + 1 < NBLK:
            unproject_rows(block + 1)
        carry = earlier_rows(block, carry)
    shift_sum, scale_sum, embed_sum = carry
    sums[...] = sums1_ref[...]
    sums[0:1, :] = shift_sum
    sums[1:2, :] = scale_sum
    sums[6:7, :] = embed_sum
    total = jnp.concatenate([sums[:, 0:HALF], sums[:, HALF:D]], axis=0).astype(BF)
    keep_ref[:, 0:HALF] = total
    send_ref[:, 0:HALF] = total
    first_half = core == 0
    chip_rows = dx0.at[pl.ds(pl.multiple_of(chip * 2 * CAP, 8), 2 * CAP)]
    lower = chip_rows[0:16, :]
    upper = chip_rows[CAP - 4 : 2 * CAP, :]
    upper = jnp.concatenate([upper[4:16], upper[0:4]], axis=0)
    keep_ref[:, HALF : 3 * HALF] = jnp.where(first_half, lower, upper).astype(BF)
    send_ref[:, HALF : 3 * HALF] = jnp.where(first_half, upper, lower).astype(BF)


def last(dq, dk, dv, h, sums1, embeds, mods, wq, wk, wv):
    packed = sds((16, 3 * HALF), BF)
    return call(
        last_kernel,
        (packed, packed),
        [VSPEC] * 10,
        [pltpu.VMEM((SLOTS, D), F32), pltpu.VMEM((8, D), F32)],
        16,
    )(dq, dk, dv, h, sums1, embeds, mods, wq, wk, wv)


def join_kernel(keep_ref, other_ref, left_ref, right_ref):
    core = lax.axis_index("core")
    for part, (out, start) in enumerate(((left_ref, 0), (left_ref, D), (right_ref, 0))):
        cols = slice(part * HALF, (part + 1) * HALF)
        out[:, pl.ds(pl.multiple_of(start + core * HALF, HALF), HALF)] = keep_ref[:, cols]
        out[:, pl.ds(pl.multiple_of(start + (1 - core) * HALF, HALF), HALF)] = other_ref[:, cols]
    shared = slice(3 * HALF, 5 * HALF)
    both = keep_ref[:, shared].astype(F32) + other_ref[:, shared].astype(F32)
    right_ref[:, D : 2 * D] = both.astype(BF)


def join(keep, other):
    half = sds((16, 2 * D), BF)
    return call(join_kernel, (half, half), [VSPEC, VSPEC])(keep, other)


def total_kernel(keep_ref, other_ref, out_ref):
    both = keep_ref[:, 0:HALF].astype(F32) + other_ref[:, 0:HALF].astype(F32)
    out_ref[...] = both.astype(BF)


def total(keep, other):
    return call(total_kernel, (sds((16, HALF), BF),), [VSPEC, VSPEC])(keep, other)[0]


def hidden_kernel(keep_ref, other_ref, mine_ref, rows_ref, picker_ref, cot_ref, embeds_ref, mods_ref, out_ref):
    cols = slice(HALF, 3 * HALF)
    dx = keep_ref[:, cols].astype(F32) + other_ref[:, cols].astype(F32)
    dx = dx[0:CAP]
    factor, normed = norm_rows(rows_ref[...].astype(F32)[0:CAP] + embeds_ref[0:1, :])
    dn = dx * (1.0 + mods_ref[1, 0:1, :])
    du = factor * (dn - normed * jnp.mean(dn * normed, axis=-1, keepdims=True))
    rows = jnp.concatenate([mine_ref[...] + du, jnp.zeros((16 - CAP, D), F32)], axis=0).astype(BF)
    picker = picker_ref[...]
    placed = tn(picker, rows)
    taken = tn(picker, jnp.ones((16, 128), BF))
    taken = jnp.concatenate([taken] * 8, axis=1)
    out_ref[0] = jnp.where(taken > 0.5, placed.astype(BF), cot_ref[0])


def hidden_grad(keep, other, mine, rows, picker, cot, embeds, mods):
    specs = [VSPEC] * 5 + [LOAD] + [VSPEC] * 2
    return call(hidden_kernel, (sds((1, TOK, D), BF),), specs, pinned=False)(
        keep, other, mine, rows, picker, cot, embeds, mods
    )[0]


def swap_cores(x):
    return lax.ppermute(x, "core", [(0, 1), (1, 0)])


def chip_index():
    return (lax.axis_index("zl") * 4 + lax.axis_index("x")) * 4 + lax.axis_index("y")


def sequence_work(gathered, rows, picker, cot, embeds, mods, weights):
    wq, wk, wv, wo = weights
    mods = mods.transpose(1, 0, 2)
    other = swap_cores(gathered)
    q, k, v, o, lse, h, g, level, x, wq, wk, wv, wo = first(gathered, other, embeds, mods, wq, wk, wv, wo)
    o_other = swap_cores(o)
    dy1, do1 = upstream_grads(g, level, mods, wo)
    dx, h1, y0, x1, o1, dq1, dk1, dv1 = second(o, o_other, h, level, do1, embeds, mods, wq, wk, wv, wo)
    dx_other = swap_cores(dx)
    grads1, gate1 = second_sums(x1, o1, dy1, dq1, dk1, dv1, g, level, wo)
    keep, send, mine, sums1, dq0, dk0, dv0 = third(
        dx, dx_other, h1, x, g, level, y0, q, k, v, o, lse, grads1, gate1, embeds, mods, wo
    )
    left, right = join(keep, swap_cores(send))
    keep_rows, send_rows = last(dq0, dk0, dv0, h, sums1, embeds, mods, wq, wk, wv)
    other_rows = swap_cores(send_rows)
    hidden = hidden_grad(keep_rows, other_rows, mine, rows, picker, cot, embeds, mods)
    return left, right, total(keep_rows, other_rows), hidden


def pair_kernel(left_ref, left_other_ref, right_ref, right_other_ref, sums_ref, sums_other_ref, left_out, right_out):
    left_out[:, 0 : 2 * D] = (left_ref[...].astype(F32) + left_other_ref[...].astype(F32)).astype(BF)
    left_out[:, 2 * D :] = (sums_ref[...].astype(F32) + sums_other_ref[...].astype(F32)).astype(BF)
    right_out[...] = (right_ref[...].astype(F32) + right_other_ref[...].astype(F32)).astype(BF)


def final_kernel(
    left_ref, left_other_ref, right_ref, right_other_ref,
    gq_ref, gk_ref, gv_ref, go_ref, embeds_ref, mods_ref,
):
    left = left_ref[...].astype(F32) + left_other_ref[...].astype(F32)
    right = right_ref[...].astype(F32) + right_other_ref[...].astype(F32)
    gq_ref[...] = left[:, 0:D]
    gk_ref[...] = left[:, D : 2 * D]
    gv_ref[...] = right[:, 0:D]
    go_ref[...] = right[:, D : 2 * D]
    sums = jnp.concatenate([left[0:8, 2 * D :], left[8:16, 2 * D :]], axis=1)
    for kind in range(3):
        for section in range(2):
            row = 3 * section + kind
            mods_ref[kind, section : section + 1, :] = sums[row : row + 1]
    embeds_ref[...] = sums[6:8]


def dp_sum(left, right, sums):
    def swap(x, far):
        return lax.ppermute(x, "dp", [(i, i ^ far) for i in range(4)])

    left, right = call(pair_kernel, (sds((16, 2 * D + HALF), BF), sds((16, 2 * D), BF)), [VSPEC] * 6)(
        left, swap(left, 1), right, swap(right, 3), sums, swap(sums, 1)
    )
    block = sds((16, D), F32)
    return call(
        final_kernel,
        (block, block, block, block, sds((2, D), F32), sds((3, 2, D), F32)),
        [VSPEC] * 4,
        pinned=False,
    )(left, swap(left, 3), right, swap(right, 1))


def shards(hidden, depth, cotangent, embeds, mods, w_query, w_key, w_value, w_out):
    payload, picker, rows = pick(depth, hidden, cotangent)
    spread = jnp.broadcast_to(payload[None], (CHIPS, PACKED, 128))
    gathered = lax.all_to_all(spread, ("zl", "x", "y"), 0, 0, tiled=True)
    left, right, sums, grad_hidden = sequence_work(
        gathered, rows, picker, cotangent, embeds, mods, (w_query, w_key, w_value, w_out)
    )
    gq, gk, gv, go, grad_embeds, grad_mods = dp_sum(left, right, sums)
    return (grad_hidden, gq, gk, gv, go, grad_embeds, grad_mods.transpose(1, 0, 2))


def solution(mesh):
    split = Mesh(mesh.devices.reshape(2, 4, 4, 2, 4), ("zl", "x", "y", "core", "dp"))
    ctx = ("zl", "x", "y", "core")
    in_specs = (P("dp", ctx, None), P("dp", ctx), P("dp", ctx, None)) + (P(),) * 6
    out_specs = (P("dp", ctx, None),) + (P(ctx, None),) * 4 + (P(), P())
    return jax.shard_map(shards, mesh=split, in_specs=in_specs, out_specs=out_specs, check_vma=False)
```
